128 devices in a mesh: lat: 8 (over z_lo, y), lon: 16 (over x, z_hi, core).
Axes of the slice: x: 4, y: 4, z: 4 (z_hi: 2, z_lo: 2; z = z_hi * 2 + z_lo), core: 2. Of those that a mesh axis runs over, the one named last changes fastest.
Arguments:
- warmth_offset: float32 [8, 512, 2048], P(None, 'lat', 'lon'), may hold values from -8 to 8
- saltiness_offset: float32 [8, 512, 2048], P(None, 'lat', 'lon'), may hold values from -2.5 to 2.5
- easterly_speed_field: float32 [8, 512, 2048], P(None, 'lat', 'lon'), may hold values from -2.5 to 2.5
- northerly_speed_field: float32 [8, 512, 2048], P(None, 'lat', 'lon'), may hold values from -2.5 to 2.5
- east_west_spacing: float32 [512, 2048], P('lat', 'lon'), may hold values from 0.7 to 1.4
- north_south_spacing: float32 [512, 2048], P('lat', 'lon'), may hold values from 0.7 to 1.4
- layer_depth_span: float32 [8, 512, 2048], P(None, 'lat', 'lon'), may hold values from 0.7 to 1.4
- water_indicator: int32 [8, 512, 2048], P(None, 'lat', 'lon'), may hold values 0 or 1
- hinge_category: int32 [1], replicated, may hold values from 0 to 1
Outputs:
- temperature_next: float32 [8, 512, 2048], P(None, 'lat', 'lon')
- salinity_next: float32 [8, 512, 2048], P(None, 'lat', 'lon')
- zonal_next: float32 [8, 512, 2048], P(None, 'lat', 'lon')
- north_next: float32 [8, 512, 2048], P(None, 'lat', 'lon')
- density: float32 [8, 512, 2048], P(None, 'lat', 'lon')
The draws below stay inside these ranges and needn't reach their ends.
Inputs may be any that keep to these rules, and one draw needn't show every extreme that they name: `water_indicator`: 1 marks sea, 0 land. `hinge_category`: 0: the row beyond the north edge mirrors the top row; 1: it mirrors the row below the top row.
All inputs are finite; a program needn't handle non-finite values. No bound on the sum of `water_indicator` on one device may be relied on, other than what follows from the above.
Results may differ from the reference program's by a relative error of at most 0.0003.
Values sent between devices are 32-bit elements; how exact they have to be, the bound alone decides.
No kernel may reach another device: no remote copies, remote signals or barrier semaphores. Data moves between devices by JAX's collectives and lax.ppermute only.
A program may use at most 64 MiB of HBM per device.

```python
import math
import jax
import jax.numpy as jnp
from jax import lax

STRATUM_TOTAL = 8
NSTEP = 4
SECTOR_TOTAL = 2048
PARALLEL_TOTAL = 512


def touch_ends(result, key, low, top_value):
    longest = result.shape.index(max(result.shape))
    spots = []
    for shift in (0, 1):
        where = [jax.random.randint(jax.random.fold_in(key, axis), (), 0, length) for axis, length in enumerate(result.shape)]
        where[longest] = (where[longest] + shift) % result.shape[longest]
        spots.append(tuple(where))
    return result.at[spots[0]].set(low).at[spots[1]].set(top_value)


def block_scale(key, extent, pieces, least, top_value):
    def one(dim, blocks):
        heights = jax.random.uniform(jax.random.fold_in(jax.random.fold_in(key, 6), dim), (blocks,), jnp.float32, least / len(pieces), top_value / len(pieces))
        return jnp.repeat(jnp.exp(heights), extent[dim] // blocks).reshape((-1,) + (1,) * (len(extent) - dim - 1))

    gain = one(*pieces[0])
    for cut in pieces[1:]:
        gain = gain * one(*cut)
    return gain


def scatter_about(own_key, extent, scale, reach, split=(), kind=jnp.bfloat16):
    loudness = block_scale(own_key, extent, split, -0.22, 0.18) if split else 1.0
    drawn = jax.random.normal(own_key, extent, jnp.float32) * scale * loudness
    return jnp.minimum(jnp.maximum(drawn, -reach), reach).astype(kind)


def setup_inputs(seed: int = 0) -> dict:
    key_of = jax.random.split(jax.random.key(seed), 10)
    return {
        "warmth_offset": scatter_about(key_of[0], (STRATUM_TOTAL, PARALLEL_TOTAL, SECTOR_TOTAL), 2.0, 8.0, ((1, 8), (2, 16)), jnp.float32),
        "saltiness_offset": scatter_about(key_of[1], (STRATUM_TOTAL, PARALLEL_TOTAL, SECTOR_TOTAL), 0.5, 2.5, ((1, 8), (2, 16)), jnp.float32),
        "easterly_speed_field": scatter_about(key_of[2], (STRATUM_TOTAL, PARALLEL_TOTAL, SECTOR_TOTAL), 0.3, 2.5, ((1, 8), (2, 16)), jnp.float32),
        "northerly_speed_field": scatter_about(key_of[3], (STRATUM_TOTAL, PARALLEL_TOTAL, SECTOR_TOTAL), 0.3, 2.5, ((1, 8), (2, 16)), jnp.float32),
        "east_west_spacing": jnp.clip(jnp.exp(math.log(1.4) - 0.6931472 * jax.random.uniform(key_of[4], (PARALLEL_TOTAL, SECTOR_TOTAL), jnp.float32) ** block_scale(key_of[4], (PARALLEL_TOTAL, SECTOR_TOTAL), ((0, 8), (1, 16)), -0.2, 0.2)), 0.7, 1.4),
        "north_south_spacing": jnp.clip(jnp.exp(math.log(1.4) - 0.6931472 * jax.random.uniform(key_of[5], (PARALLEL_TOTAL, SECTOR_TOTAL), jnp.float32) ** block_scale(key_of[5], (PARALLEL_TOTAL, SECTOR_TOTAL), ((0, 8), (1, 16)), -0.2, 0.2)), 0.7, 1.4),
        "layer_depth_span": jnp.clip(jnp.exp(math.log(1.4) - 0.6931472 * jax.random.uniform(key_of[6], (STRATUM_TOTAL, PARALLEL_TOTAL, SECTOR_TOTAL), jnp.float32) ** block_scale(key_of[6], (STRATUM_TOTAL, PARALLEL_TOTAL, SECTOR_TOTAL), ((1, 8), (2, 16)), -0.2, 0.2)), 0.7, 1.4),
        "water_indicator": touch_ends((jax.random.randint(key_of[7], (STRATUM_TOTAL, PARALLEL_TOTAL, SECTOR_TOTAL), 0, 4) < 3).astype(jnp.int32), jax.random.fold_in(key_of[7], 1), 0, 1),
        "hinge_category": jax.random.randint(key_of[8], (1,), 0, 2).astype(jnp.int32),
    }


time_step = 0.2
diffusivity = 0.4
eos_alpha = 1.6550e-1
eos_beta = 7.6554e-1
eos_lambda_one = 5.9520e-2
eos_lambda_two = 5.4914e-4
eos_mu_one = 1.4970e-4
eos_mu_two = 1.1090e-5
eos_cross = 2.4341e-3


def density_of(heat, salt, depth):
    return (-eos_alpha * (1.0 + 0.5 * eos_lambda_one * heat + eos_mu_one * depth) * heat
            + eos_beta * (1.0 - 0.5 * eos_lambda_two * salt - eos_mu_two * depth) * salt
            - eos_cross * heat * salt)


def extend(fields, signs, hinge_category):
    wrapped = jnp.concatenate([fields[:, :, -1:], fields, fields[:, :, :1]], axis=2)
    source_row = (PARALLEL_TOTAL - 1 - hinge_category[0]).astype(jnp.int32)
    source = lax.dynamic_index_in_dim(wrapped, source_row, 1, False)
    north_ghost = jnp.flip(source, axis=1) * signs[:, None]
    south_ghost = jnp.zeros_like(north_ghost)
    return jnp.concatenate([south_ghost[:, None, :], wrapped, north_ghost[:, None, :]], axis=1)


def face_geometry(metric_halo):
    east_scale = metric_halo[0]
    north_scale = metric_halo[1]
    depth_cell = metric_halo[2:]
    open_cell = (depth_cell > 0.0).astype(jnp.float32)
    east_span = 0.5 * (east_scale[1:-1, :-1] + east_scale[1:-1, 1:])
    east_side = 0.5 * (north_scale[1:-1, :-1] + north_scale[1:-1, 1:])
    east_depth = 0.5 * (depth_cell[:, 1:-1, :-1] + depth_cell[:, 1:-1, 1:])
    open_east = open_cell[:, 1:-1, :-1] * open_cell[:, 1:-1, 1:]
    area_east = east_side * east_depth * open_east
    conduct_east = diffusivity * area_east / east_span
    north_span = 0.5 * (north_scale[:-1, 1:-1] + north_scale[1:, 1:-1])
    north_side = 0.5 * (east_scale[:-1, 1:-1] + east_scale[1:, 1:-1])
    north_depth = 0.5 * (depth_cell[:, :-1, 1:-1] + depth_cell[:, 1:, 1:-1])
    open_north = open_cell[:, :-1, 1:-1] * open_cell[:, 1:, 1:-1]
    area_north = north_side * north_depth * open_north
    conduct_north = diffusivity * area_north / north_span
    return (area_east, conduct_east, area_north, conduct_north, open_east, open_north,
            east_span, north_span, depth_cell)


def advance(halo_all, geometry, inv_volume, wet, depth, stratum_total):
    (area_east, conduct_east, area_north, conduct_north, open_east, open_north,
     east_span, north_span, depth_cell) = geometry
    heat_halo = halo_all[:stratum_total]
    salt_halo = halo_all[stratum_total:2 * stratum_total]
    east_halo = halo_all[2 * stratum_total:3 * stratum_total]
    north_halo = halo_all[3 * stratum_total:]
    flow_east = area_east * east_halo[:, 1:-1, :-1]
    flow_north = area_north * north_halo[:, :-1, 1:-1]

    def tendency(field):
        west_cell = field[:, 1:-1, :-1]
        east_cell = field[:, 1:-1, 1:]
        flux_east = (jnp.maximum(flow_east, 0.0) * west_cell + jnp.minimum(flow_east, 0.0) * east_cell
                     - conduct_east * (east_cell - west_cell))
        south_cell = field[:, :-1, 1:-1]
        north_cell = field[:, 1:, 1:-1]
        flux_north = (jnp.maximum(flow_north, 0.0) * south_cell + jnp.minimum(flow_north, 0.0) * north_cell
                      - conduct_north * (north_cell - south_cell))
        return inv_volume * (flux_east[:, :, 1:] - flux_east[:, :, :-1] + flux_north[:, 1:, :] - flux_north[:, :-1, :])

    weight = density_of(heat_halo, salt_halo, depth) * depth_cell
    pressure = jnp.cumsum(weight, axis=0) - 0.5 * weight
    push_east = (pressure[:, 1:-1, :-1] - pressure[:, 1:-1, 1:]) / east_span
    push_north = (pressure[:, :-1, 1:-1] - pressure[:, 1:, 1:-1]) / north_span
    heat_new = (heat_halo[:, 1:-1, 1:-1] - tendency(heat_halo)) * wet
    salt_new = (salt_halo[:, 1:-1, 1:-1] - tendency(salt_halo)) * wet
    east_new = (east_halo[:, 1:-1, 1:-1] - tendency(east_halo) + time_step * push_east[:, :, 1:]) * open_east[:, :, 1:]
    north_new = (north_halo[:, 1:-1, 1:-1] - tendency(north_halo) + time_step * push_north[:, 1:, :]) * open_north[:, 1:, :]
    return heat_new, salt_new, east_new, north_new


def reference(warmth_offset, saltiness_offset, easterly_speed_field, northerly_speed_field, east_west_spacing, north_south_spacing, layer_depth_span, water_indicator, hinge_category):
    stratum_total = warmth_offset.shape[0]
    wet = water_indicator.astype(jnp.float32)
    metric_stack = jnp.concatenate([east_west_spacing[None], north_south_spacing[None], layer_depth_span * wet], axis=0)
    metric_halo = extend(metric_stack, jnp.ones((stratum_total + 2,), jnp.float32), hinge_category)
    geometry = face_geometry(metric_halo)
    inv_volume = time_step / (east_west_spacing * north_south_spacing * layer_depth_span)
    depth = ((jnp.arange(stratum_total).astype(jnp.float32) + 0.5) * 100.0).reshape(stratum_total, 1, 1)
    signs = jnp.concatenate([jnp.ones((2 * stratum_total,), jnp.float32), -jnp.ones((2 * stratum_total,), jnp.float32)])
    prognostic_variables = (warmth_offset, saltiness_offset, easterly_speed_field, northerly_speed_field)
    for step_index in range(NSTEP):
        halo_all = extend(jnp.concatenate(prognostic_variables, axis=0), signs, hinge_category)
        prognostic_variables = advance(halo_all, geometry, inv_volume, wet, depth, stratum_total)
    density = density_of(prognostic_variables[0], prognostic_variables[1], depth) * wet
    return prognostic_variables[0], prognostic_variables[1], prognostic_variables[2], prognostic_variables[3], density
```

```python
import jax
import jax.numpy as jnp
from jax import lax
from jax.experimental import pallas as pl
from jax.experimental.pallas import tpu as pltpu
from jax.sharding import PartitionSpec as P

F32 = jnp.float32
NSTEP = 4
LEVELS = 8
ROWS = 64
LANES = 128
HALO = 4
BLOCK = 9
GROUP = 16

time_step = 0.2
diffusivity = 0.4
eos_alpha = 0.1655
eos_beta = 0.76554
eos_lambda_one = 0.05952
eos_lambda_two = 0.00054914
eos_mu_one = 0.0001497
eos_mu_two = 1.109e-05
eos_cross = 0.0024341

SIGNS = (1.0, 1.0, -1.0, -1.0)
VMEM_LIMIT = 40 * 1024 * 1024


def roll(x, shift):
    shift = shift % LANES
    return pltpu.roll(x, shift, 1) if shift else x


def lanes():
    return lax.broadcasted_iota(jnp.int32, (LEVELS, LANES), 1)


def levels():
    return lax.broadcasted_iota(jnp.int32, (LEVELS, LANES), 0)


def mirrored(x, width):
    lane = lanes()
    bit = 1
    while bit < width:
        x = jnp.where((lane & bit) != 0, roll(x, bit), roll(x, -bit))
        bit *= 2
    return x


def eos_terms():
    depth = 100.0 * (levels().astype(F32) + 0.5)
    return -eos_alpha * (1.0 + eos_mu_one * depth), eos_beta * (1.0 - eos_mu_two * depth)


def density_of(heat, salt, terms):
    heat_term, salt_term = terms
    return heat * (heat_term - (0.5 * eos_alpha * eos_lambda_one) * heat - eos_cross * salt) + salt * (
        salt_term - (0.5 * eos_beta * eos_lambda_two) * salt
    )


def pressure_of(heat, salt, half_depth, terms):
    half = density_of(heat, salt, terms) * half_depth
    level = levels()
    total = half
    for shift in (1, 2, 4):
        total = total + jnp.where(level >= shift, pltpu.roll(total, shift, 0), 0.0)
    return total + total - half


def geometry_row(geo, row, east0, north0, east1, north1):
    half0 = geo["half"][row]
    half1 = geo["half"][row + 1]
    half_e = roll(half0, -1)
    span = 2.0 / (east0 + roll(east0, -1))
    side = 0.5 * (north0 + roll(north0, -1))
    open_e = jnp.minimum(half0, half_e) > 0.0
    area = jnp.where(open_e, side * (half0 + half_e), 0.0)
    geo["area_e"][row] = area
    geo["cond_e"][row] = diffusivity * area * span
    geo["open_e"][row] = jnp.where(open_e, 1.0, 0.0)
    geo["push_e"][row] = time_step * span
    span = 2.0 / (north0 + north1)
    side = 0.5 * (east0 + east1)
    open_n = jnp.minimum(half0, half1) > 0.0
    area = jnp.where(open_n, side * (half0 + half1), 0.0)
    geo["area_n"][row] = area
    geo["cond_n"][row] = diffusivity * area * span
    geo["open_n"][row] = jnp.where(open_n, 1.0, 0.0)
    geo["push_n"][row] = time_step * span
    geo["inv"][row] = (0.5 * time_step) / (east0 * north0 * jnp.where(half0 > 0.0, half0, 1.0))


def march(state, geo, bases, low, blocks, unroll):
    terms = eos_terms()

    def north_face(row, speed):
        flow = geo["area_n"][row] * speed
        ahead = jnp.maximum(flow, 0.0) + geo["cond_n"][row]
        return ahead, flow - ahead

    def first(base):
        row = base + low
        before = tuple(ref[row - 1] for ref in state)
        here = tuple(ref[row] for ref in state)
        return before + here + north_face(row - 1, before[3]) + (pressure_of(here[0], here[1], geo["half"][row], terms),)

    def block(index, carries):
        start = low + index * unroll
        nexts = [[tuple(ref[base + start + u + 1] for ref in state) for u in range(unroll)] for base in bases]
        after = []
        stores = []
        for base, ahead_rows, carry in zip(bases, nexts, carries):
            before, here = carry[0:4], carry[4:8]
            south_p, south_m, press = carry[8:]
            for u in range(unroll):
                row = base + start + u
                north = ahead_rows[u]
                press_n = pressure_of(north[0], north[1], geo["half"][row + 1], terms)
                north_p, north_m = north_face(row, here[3])
                flow = geo["area_e"][row] * here[2]
                east_p = jnp.maximum(flow, 0.0) + geo["cond_e"][row]
                east_m = flow - east_p
                west_p, west_m = roll(east_p, 1), roll(east_m, 1)
                inv = geo["inv"][row]
                keep = 1.0 - inv * ((east_p - west_m) + (north_p - south_m))
                c_e, c_w, c_n, c_s = inv * east_m, inv * west_p, inv * north_m, inv * south_p
                new = [
                    keep * c + (c_w * roll(c, 1) + c_s * s) - (c_e * roll(c, -1) + c_n * n)
                    for c, s, n in zip(here, before, north)
                ]
                new[2] = (new[2] + (press - roll(press, -1)) * geo["push_e"][row]) * geo["open_e"][row]
                new[3] = (new[3] + (press - press_n) * geo["push_n"][row]) * geo["open_n"][row]
                stores.append((row, new))
                before, here = here, north
                south_p, south_m, press = north_p, north_m, press_n
            after.append(before + here + (south_p, south_m, press))
        for row, new in stores:
            for ref, value in zip(state, new):
                ref[row] = value
        return tuple(after)

    lax.fori_loop(0, blocks, block, tuple(first(base) for base in bases))


GEO = ("half", "area_e", "cond_e", "open_e", "push_e", "area_n", "cond_n", "open_n", "push_n", "inv")


def geo_scratch(rows):
    return [pltpu.VMEM((rows, LEVELS, LANES), F32) for _ in GEO]


def column_of(ref, row):
    return ref[pl.ds(row, LEVELS, stride=ROWS), :]


def wide(ref, row):
    return jnp.broadcast_to(ref[pl.ds(row, 1), :], (LEVELS, LANES))


def own_row(refs, row):
    heat, salt, east, north, thick, water = [column_of(ref, row) for ref in refs[:6]]
    wet = water.astype(F32)
    return heat * wet, salt * wet, east, north, 0.5 * (thick * wet)


def rows_kernel(*refs):
    ins, (out_a, out_b) = refs[:8], refs[8:]
    even = lax.rem(lax.axis_index("lat"), 2) == 0
    start_a = jnp.where(even, ROWS - HALO, 0)
    start_b = jnp.where(even, 0, ROWS - HALO - 1)
    out_b[25] = jnp.ones((LEVELS, LANES), F32)
    out_b[26] = jnp.ones((LEVELS, LANES), F32)
    for i in range(HALO):
        for f, value in enumerate(own_row(ins, start_a + i)):
            out_a[5 * i + f] = value
        out_a[20, pl.ds(i, 1), :] = ins[6][pl.ds(start_a + i, 1), :]
        out_a[20, pl.ds(HALO + i, 1), :] = ins[7][pl.ds(start_a + i, 1), :]
    for i in range(HALO + 1):
        for f, value in enumerate(own_row(ins, start_b + i)):
            out_b[5 * i + f] = value
        out_b[25, pl.ds(i, 1), :] = ins[6][pl.ds(start_b + i, 1), :]
        out_b[26, pl.ds(i, 1), :] = ins[7][pl.ds(start_b + i, 1), :]


def halo_rows(got_a, got_b):
    even = lax.rem(lax.axis_index("lat"), 2) == 0

    def spread(row):
        return jnp.broadcast_to(row, (LEVELS, LANES))

    def read_a(i, f):
        if f < 5:
            return got_a[5 * i + f]
        return spread(got_a[20, pl.ds(HALO * (f - 5) + i, 1), :])

    def read_b(i, f):
        if f < 5:
            return got_b[5 * i + f]
        return spread(got_b[20 + f, pl.ds(i, 1), :])

    def sane(value, f):
        return value if f < 5 else jnp.where(value > 0.0, value, 1.0)

    def south(i, f):
        return sane(jnp.where(even, read_b(i + 1, f), read_a(i, f)), f)

    def north(i, f):
        return sane(jnp.where(even, read_a(i, f), read_b(i, f)), f)

    def fold(i, f):
        return sane(read_b(i, f), f)

    return south, north, fold


def interior_kernel(*refs):
    ins = refs[:8]
    state_out, own, msgs = refs[8:11]
    state = [state_out.at[f] for f in range(4)]
    geo = dict(zip(GEO, refs[11:]))

    def take(row, carry):
        values = own_row(ins, row)
        for ref, value in zip(state, values):
            ref[row] = value
        geo["half"][row] = values[4]
        return carry

    lax.fori_loop(0, ROWS, take, 0)

    lane = lanes()
    part = (lane // HALO) % (GROUP // HALO)

    def pack(g, carry):
        packs = []
        for f in range(7):
            west = east = jnp.zeros((LEVELS, LANES), F32)
            for q in range(8):
                row = jnp.clip(BLOCK * q + g - HALO, 0, ROWS - 1)
                if f < 4:
                    value = state[f][row]
                elif f == 4:
                    value = geo["half"][row]
                else:
                    value = wide(ins[f + 1], row)
                here = (lane // GROUP) == q
                west = jnp.where(here, roll(value, GROUP * q + HALO), west)
                east = jnp.where(here, roll(value, GROUP * q + 12), east)
            own[0, f, g] = west
            own[1, f, g] = east
            packs.append((west, east))
        for side in range(2):
            for half, first in ((0, 0), (1, 4)):
                message = jnp.zeros((LEVELS, LANES), F32)
                for f in range(4 if half == 0 else 3):
                    value = packs[first + f][side]
                    shift = HALO * f - (HALO if side == 0 else 2 * HALO)
                    message = jnp.where(part == f, roll(value, shift), message)
                msgs[side, BLOCK * half + g] = message
        return carry

    lax.fori_loop(0, BLOCK, pack, 0)

    def shape(row, carry):
        geometry_row(geo, row, wide(ins[6], row), wide(ins[7], row), wide(ins[6], row + 1), wide(ins[7], row + 1))
        return carry

    lax.fori_loop(0, ROWS - 1, shape, 0)

    def step(s, carry):
        march(state, geo, (0,), s, 32 - s, 2)
        return carry

    lax.fori_loop(1, NSTEP + 1, step, 0)


def columns_kernel(msgs, got_a, got_b, out_a, out_b):
    even = lax.rem(lax.axis_index("lon"), 2) == 0
    top = lax.axis_index("lat") == lax.axis_size("lat") - 1
    south, north, fold = halo_rows(got_a, got_b)
    lane = lanes()
    part = (lane // HALO) % (GROUP // HALO)
    for half, first in ((0, 0), (1, 4)):
        for g in range(BLOCK):
            slot = BLOCK * half + g
            west, east = msgs[0, slot], msgs[1, slot]
            if g != HALO:
                add_w = add_e = jnp.zeros((LEVELS, LANES), F32)
                base = 0 if g < HALO else 7 * GROUP
                for f in range(4 if half == 0 else 3):
                    if g < HALO:
                        value = south(g, first + f)
                    else:
                        value = jnp.where(top, fold(g - 4, first + f), north(g - 5, first + f))
                    add_w = jnp.where(part == f, roll(value, base + HALO * f), add_w)
                    add_e = jnp.where(part == f, roll(value, base + HALO * f + HALO), add_e)
                if g < HALO:
                    here = lane < GROUP
                else:
                    here = lane >= 7 * GROUP
                    add_w, add_e = jnp.where(top, add_e, add_w), jnp.where(top, add_w, add_e)
                west = jnp.where(here, add_w, west)
                east = jnp.where(here, add_e, east)
            out_a[slot] = jnp.where(even, east, west)
            out_b[slot] = jnp.where(even, west, east)


SOUTH, NORTH, FOLD, NS_ROWS = 0, 12, 24, 30


def rows_strip_kernel(*refs):
    ins = refs[:8]
    got_a, got_b, hinge, out = refs[8:12]
    state = refs[12:16]
    east_w, north_w = refs[16:18]
    geo = dict(zip(GEO, refs[18:]))
    top = lax.axis_index("lat") == lax.axis_size("lat") - 1
    pivot = hinge[0]
    south, north, fold = halo_rows(got_a, got_b)
    fields = list(state) + [geo["half"], east_w, north_w]
    for i in range(HALO):
        for f, ref in enumerate(fields):
            ref[SOUTH + i] = south(i, f)
            ref[NORTH + 8 + i] = north(i, f)
    for i in range(8):
        for base, row in ((SOUTH + HALO, i), (NORTH, ROWS - 8 + i)):
            for ref, value in zip(fields, own_row(ins, row) + (wide(ins[6], row), wide(ins[7], row))):
                ref[base + i] = value

    def refold(ref, sign):
        ghost = sign * mirrored(ref[FOLD + 4 - pivot], LANES)
        ref[FOLD + 5] = sign * mirrored(ref[NORTH + 7 - pivot], LANES)
        ref[NORTH + 8] = ghost

    def shape(row, carry):
        geometry_row(geo, row, east_w[row], north_w[row], east_w[row + 1], north_w[row + 1])
        return carry

    @pl.when(top)
    def _():
        for i in range(HALO + 1):
            for f, ref in enumerate(fields):
                ref[FOLD + i] = fold(i, f)
        for ref in fields[4:]:
            refold(ref, 1.0)
        lax.fori_loop(FOLD, FOLD + 5, shape, 0)

    lax.fori_loop(SOUTH, SOUTH + 11, shape, 0)
    lax.fori_loop(NORTH, NORTH + 11, shape, 0)

    def step(s, carry):
        @pl.when(top)
        def _():
            for ref, sign in zip(state, SIGNS):
                refold(ref, sign)
            march(state, geo, (FOLD,), s, 5 - s, 1)

        march(state, geo, (SOUTH, NORTH), s, 6 - s, 2)
        return carry

    lax.fori_loop(1, NSTEP + 1, step, 0)
    for f, ref in enumerate(state):
        for i in range(HALO):
            out[f, i] = ref[SOUTH + HALO + i]
            out[f, HALO + i] = ref[NORTH + HALO + i]


WEST, EAST, FOLDS, WE_ROWS = 0, 11, 22, 28


def columns_strip_kernel(*refs):
    own, lon_a, lon_b, got_a, got_b, inner, strips, hinge = refs[:8]
    outs = refs[8:13]
    state = refs[13:17]
    east_w, north_w = refs[17:19]
    geo = dict(zip(GEO, refs[19:]))
    even = lax.rem(lax.axis_index("lon"), 2) == 0
    top = lax.axis_index("lat") == lax.axis_size("lat") - 1
    pivot = hinge[0]
    south, north, fold = halo_rows(got_a, got_b)
    fields = list(state) + [geo["half"], east_w, north_w]
    lane = lanes()
    inside = lane % GROUP

    def message(side, f, g):
        slot = g if f < 4 else BLOCK + g
        a, b = lon_a[slot], lon_b[slot]
        return jnp.where(even, b, a) if side == 0 else jnp.where(even, a, b)

    for g in range(BLOCK):
        for f, ref in enumerate(fields):
            west, east = own[0, f, g], own[1, f, g]
            if g < HALO:
                value = south(g, f)
                west = jnp.where(lane < GROUP, roll(value, HALO), west)
                east = jnp.where(lane < GROUP, roll(value, 12), east)
            elif g > HALO:
                value = north(g - 5, f)
                west = jnp.where(lane >= 7 * GROUP, roll(value, 7 * GROUP + HALO), west)
                east = jnp.where(lane >= 7 * GROUP, roll(value, 7 * GROUP + 12), east)
            shift = -HALO * (f % 4)
            west = jnp.where(inside < HALO, roll(message(0, f, g), shift), west)
            east = jnp.where(inside >= 12, roll(message(1, f, g), shift + 12), east)
            if f > 4:
                west = jnp.where(west > 0.0, west, 1.0)
                east = jnp.where(east > 0.0, east, 1.0)
            ref[WEST + 1 + g] = west
            ref[EAST + 1 + g] = east

    def rewrap(ref):
        for base in (WEST, EAST):
            ref[base] = roll(ref[base + 9], GROUP)
            ref[base + 10] = roll(ref[base + 1], -GROUP)

    def refold(ref, sign):
        ghost = sign * mirrored(ref[FOLDS + 4 - pivot], GROUP)
        from_e, from_w = ref[EAST + 5 - pivot], ref[WEST + 5 - pivot]
        back = jnp.where(lane < GROUP, roll(from_e, GROUP), roll(from_w, 2 * GROUP))
        ref[FOLDS + 5] = sign * mirrored(back, GROUP)
        here = lane >= 7 * GROUP
        ref[WEST + 6] = jnp.where(here, roll(ghost, 6 * GROUP), ref[WEST + 6])
        ref[EAST + 6] = jnp.where(here, roll(ghost, 7 * GROUP), ref[EAST + 6])

    def shape(row, carry):
        geometry_row(geo, row, east_w[row], north_w[row], east_w[row + 1], north_w[row + 1])
        return carry

    @pl.when(top)
    def _():
        for i in range(HALO + 1):
            for f, ref in enumerate(fields):
                value = fold(i, f)
                value = jnp.where(lane < GROUP, roll(value, HALO), roll(value, 28))
                if i > 0:
                    slot = HALO + i
                    corner = 7 * GROUP + HALO * (f % 4)
                    value = jnp.where(lane < HALO, roll(message(1, f, slot), -corner), value)
                    other = roll(message(0, f, slot), 28 - corner)
                    value = jnp.where((lane >= 28) & (lane < 32), other, value)
                if f > 4:
                    value = jnp.where(value > 0.0, value, 1.0)
                ref[FOLDS + i] = value
        for ref in fields[4:]:
            refold(ref, 1.0)

    for ref in fields[4:]:
        rewrap(ref)

    lax.fori_loop(WEST, WEST + 10, shape, 0)
    lax.fori_loop(EAST, EAST + 10, shape, 0)

    @pl.when(top)
    def _():
        lax.fori_loop(FOLDS, FOLDS + 5, shape, 0)

    def step(s, carry):
        @pl.when(top)
        def _():
            for ref, sign in zip(state, SIGNS):
                refold(ref, sign)
            march(state, geo, (FOLDS,), s, 5 - s, 1)

        for ref in state:
            rewrap(ref)
        march(state, geo, (WEST, EAST), 1, 3, 3)
        return carry

    lax.fori_loop(1, NSTEP + 1, step, 0)

    for ref in state:
        for g in range(BLOCK):
            ref[WEST + 1 + g] = jnp.where(inside < HALO, roll(ref[EAST + 1 + g], -8), ref[WEST + 1 + g])
    rim = (lane < HALO) | (lane >= LANES - HALO)
    terms = eos_terms()

    def emit(row, bases, q, g):
        new = [
            jnp.where(rim, roll(ref[WEST + 1 + g], -(GROUP * q + HALO)), base) for ref, base in zip(state, bases)
        ]
        new.append(density_of(new[0], new[1], terms))
        for ref, value in zip(outs, new):
            ref[pl.ds(row, LEVELS, stride=ROWS), :] = value

    for i in range(HALO):
        emit(i, [strips[f, i] for f in range(4)], 0, HALO + i)
        emit(ROWS - HALO + i, [strips[f, HALO + i] for f in range(4)], 7, 1 + i)
    emit(HALO, [inner[f, HALO] for f in range(4)], 0, 8)
    emit(ROWS - HALO - 1, [inner[f, ROWS - HALO - 1] for f in range(4)], 7, 0)

    def merge(g, carry):
        for q in range(1, 7):
            row = BLOCK * q + g - HALO
            emit(row, [inner[f, row] for f in range(4)], q, g)
        return carry

    lax.fori_loop(0, BLOCK, merge, 0)


def call(kernel, ins, outs, scratch=(), smem_last=False, flops=0):
    specs = [pl.BlockSpec(memory_space=pltpu.VMEM) for _ in ins]
    if smem_last:
        specs[-1] = pl.BlockSpec(memory_space=pltpu.SMEM)
    return pl.pallas_call(
        kernel,
        out_shape=[jax.ShapeDtypeStruct(shape, F32) for shape in outs],
        in_specs=specs,
        out_specs=[pl.BlockSpec(memory_space=pltpu.VMEM) for _ in outs],
        scratch_shapes=list(scratch),
        compiler_params=pltpu.CompilerParams(vmem_limit_bytes=VMEM_LIMIT),
        cost_estimate=pl.CostEstimate(flops=flops, bytes_accessed=2_000_000, transcendentals=0),
    )(*ins)


def lat_pairs(lat, lon):
    first = [(a * lon + o, (a ^ 1) * lon + o) for a in range(lat) for o in range(lon)]
    second = [
        (a * lon + o, (a + 1 if a % 2 else a - 1) * lon + o) for a in range(1, lat - 1) for o in range(lon)
    ]
    second += [((lat - 1) * lon + o, (lat - 1) * lon + lon - 1 - o) for o in range(lon)]
    return first, second


def lon_pairs(lat, lon):
    first = [(a * lon + o, a * lon + (o ^ 1)) for a in range(lat) for o in range(lon)]
    second = [
        (a * lon + o, a * lon + ((o + 1) if o % 2 else (o - 1)) % lon) for a in range(lat) for o in range(lon)
    ]
    return first, second


def on_device(*args):
    lat, lon = lax.axis_size("lat"), lax.axis_size("lon")
    axes = ("lat", "lon")
    flat = [x.reshape(LEVELS * ROWS, LANES) for x in (*args[:4], args[6], args[7])]
    ins = flat + [args[4], args[5]]
    hinge = args[8]
    tile = (LEVELS, LANES)
    state_scratch = lambda rows: [pltpu.VMEM((rows,) + tile, F32) for _ in range(6)]

    rows_a, rows_b = call(rows_kernel, ins, [(21,) + tile, (27,) + tile])
    pairs_a, pairs_b = lat_pairs(lat, lon)
    got_b = lax.ppermute(rows_b, axes, pairs_b)
    got_a = lax.ppermute(rows_a, axes, pairs_a)
    inner, own, msgs = call(
        interior_kernel,
        ins,
        [(4, ROWS) + tile, (2, 7, BLOCK) + tile, (2, 2 * BLOCK) + tile],
        geo_scratch(ROWS),
        flops=40_000_000,
    )
    cols_a, cols_b = call(columns_kernel, [msgs, got_a, got_b], [(2 * BLOCK,) + tile] * 2)
    pairs_a, pairs_b = lon_pairs(lat, lon)
    lon_b = lax.ppermute(cols_b, axes, pairs_b)
    lon_a = lax.ppermute(cols_a, axes, pairs_a)
    (strips,) = call(
        rows_strip_kernel,
        ins + [got_a, got_b, hinge],
        [(4, 2 * HALO) + tile],
        state_scratch(NS_ROWS) + geo_scratch(NS_ROWS),
        smem_last=True,
        flops=10_000_000,
    )
    outs = call(
        columns_strip_kernel,
        [own, lon_a, lon_b, got_a, got_b, inner, strips, hinge],
        [(LEVELS * ROWS, LANES)] * 5,
        state_scratch(WE_ROWS) + geo_scratch(WE_ROWS),
        smem_last=True,
        flops=10_000_000,
    )
    return tuple(x.reshape(LEVELS, ROWS, LANES) for x in outs)


def solution(mesh):
    field = P(None, "lat", "lon")
    flat = P("lat", "lon")
    return jax.shard_map(
        on_device,
        mesh=mesh,
        in_specs=(field, field, field, field, flat, flat, field, field, P()),
        out_specs=(field,) * 5,
        check_vma=False,
    )
```

```python
import jax
import jax.numpy as jnp
from jax import lax
from jax.experimental import pallas as pl
from jax.experimental.pallas import tpu as pltpu
from jax.sharding import PartitionSpec as P

F32 = jnp.float32
NSTEP = 4
LEVELS = 8
ROWS = 64
LANES = 128
HALO = 4
BLOCK = 9
GROUP = 16

time_step = 0.2
diffusivity = 0.4
eos_alpha = 0.1655
eos_beta = 0.76554
eos_lambda_one = 0.05952
eos_lambda_two = 0.00054914
eos_mu_one = 0.0001497
eos_mu_two = 1.109e-05
eos_cross = 0.0024341

SIGNS = (1.0, 1.0, -1.0, -1.0)
MIB = 1024 * 1024


def roll(x, shift):
    shift = shift % LANES
    return pltpu.roll(x, shift, 1) if shift else x


def lanes():
    return lax.broadcasted_iota(jnp.int32, (LEVELS, LANES), 1)


def levels():
    return lax.broadcasted_iota(jnp.int32, (LEVELS, LANES), 0)


def mirrored(x, width):
    lane = lanes()
    bit = 1
    while bit < width:
        x = jnp.where((lane & bit) != 0, roll(x, bit), roll(x, -bit))
        bit *= 2
    return x


def eos_terms():
    depth = 100.0 * (levels().astype(F32) + 0.5)
    return -eos_alpha * (1.0 + eos_mu_one * depth), eos_beta * (1.0 - eos_mu_two * depth)


def density_of(heat, salt, terms):
    heat_term, salt_term = terms
    return heat * (heat_term - (0.5 * eos_alpha * eos_lambda_one) * heat - eos_cross * salt) + salt * (
        salt_term - (0.5 * eos_beta * eos_lambda_two) * salt
    )


def pressure_of(heat, salt, half_depth, terms):
    half = density_of(heat, salt, terms) * half_depth
    level = levels()
    total = half
    for shift in (1, 2, 4):
        total = total + jnp.where(level >= shift, pltpu.roll(total, shift, 0), 0.0)
    return total + total - half


def geometry_row(geo, row, east0, north0, east1, north1):
    half0 = geo["half"][row]
    half1 = geo["half"][row + 1]
    half_e = roll(half0, -1)
    span = 2.0 / (east0 + roll(east0, -1))
    side = 0.5 * (north0 + roll(north0, -1))
    open_e = jnp.minimum(half0, half_e) > 0.0
    area = jnp.where(open_e, side * (half0 + half_e), 0.0)
    geo["area_e"][row] = area
    geo["cond_e"][row] = diffusivity * area * span
    geo["open_e"][row] = jnp.where(open_e, 1.0, 0.0)
    geo["push_e"][row] = time_step * span
    span = 2.0 / (north0 + north1)
    side = 0.5 * (east0 + east1)
    open_n = jnp.minimum(half0, half1) > 0.0
    area = jnp.where(open_n, side * (half0 + half1), 0.0)
    geo["area_n"][row] = area
    geo["cond_n"][row] = diffusivity * area * span
    geo["open_n"][row] = jnp.where(open_n, 1.0, 0.0)
    geo["push_n"][row] = time_step * span
    geo["inv"][row] = (0.5 * time_step) / (east0 * north0 * jnp.where(half0 > 0.0, half0, 1.0))


def march(state, geo, chains, unroll=None):
    terms = eos_terms()

    def north_face(row, speed):
        flow = geo["area_n"][row] * speed
        ahead = jnp.maximum(flow, 0.0) + geo["cond_n"][row]
        return ahead, flow - ahead

    def begin(row):
        before = tuple(ref[row - 1] for ref in state)
        here = tuple(ref[row] for ref in state)
        return before + here + north_face(row - 1, before[3]) + (pressure_of(here[0], here[1], geo["half"][row], terms),)

    def advance(row, carry):
        before, here = carry[0:4], carry[4:8]
        south_p, south_m, press = carry[8:]
        north = tuple(ref[row + 1] for ref in state)
        press_n = pressure_of(north[0], north[1], geo["half"][row + 1], terms)
        north_p, north_m = north_face(row, here[3])
        flow = geo["area_e"][row] * here[2]
        east_p = jnp.maximum(flow, 0.0) + geo["cond_e"][row]
        east_m = flow - east_p
        west_p, west_m = roll(east_p, 1), roll(east_m, 1)
        inv = geo["inv"][row]
        keep = 1.0 - inv * ((east_p - west_m) + (north_p - south_m))
        c_e, c_w, c_n, c_s = inv * east_m, inv * west_p, inv * north_m, inv * south_p
        new = [
            keep * c + (c_w * roll(c, 1) + c_s * s) - (c_e * roll(c, -1) + c_n * n)
            for c, s, n in zip(here, before, north)
        ]
        new[2] = (new[2] + (press - roll(press, -1)) * geo["push_e"][row]) * geo["open_e"][row]
        new[3] = (new[3] + (press - press_n) * geo["push_n"][row]) * geo["open_n"][row]
        for ref, value in zip(state, new):
            ref[row] = value
        return here + north + (north_p, north_m, press_n)

    carries = [begin(first) for first, _ in chains]
    if unroll is None:
        for u in range(max(count for _, count in chains)):
            for index, (first, count) in enumerate(chains):
                if u < count:
                    carries[index] = advance(first + u, carries[index])
    else:
        ((first, count),) = chains

        def block(index, carry):
            for u in range(unroll):
                carry = advance(first + index * unroll + u, carry)
            return carry

        lax.fori_loop(0, count // unroll, block, carries[0])


GEO = ("half", "area_e", "cond_e", "open_e", "push_e", "area_n", "cond_n", "open_n", "push_n", "inv")


def geo_scratch(rows):
    return [pltpu.VMEM((rows, LEVELS, LANES), F32) for _ in GEO]


def column_of(ref, row):
    return ref[pl.ds(row, LEVELS, stride=ref.shape[0] // LEVELS), :]


def wide(ref, row):
    return jnp.broadcast_to(ref[pl.ds(row, 1), :], (LEVELS, LANES))


def own_row(refs, row):
    heat, salt, east, north, thick, water = [column_of(ref, row) for ref in refs[:6]]
    wet = water.astype(F32)
    return heat * wet, salt * wet, east, north, 0.5 * (thick * wet)


def rows_kernel(*refs):
    ins, (out_a, out_b) = refs[:8], refs[8:10]
    rims, sems = refs[10:18], refs[18]
    copies = []
    for f, (src, dst) in enumerate(zip(ins, rims)):
        for side, row in ((0, 0), (1, ROWS - 8)):
            if f < 6:
                pair = src.at[:, pl.ds(row, 8), :], dst.at[side]
            else:
                pair = src.at[pl.ds(row, 8), :], dst.at[side]
            copies.append(pltpu.make_async_copy(*pair, sems.at[f, side]))
    for copy in copies:
        copy.start()
    out_b[25] = jnp.ones((LEVELS, LANES), F32)
    out_b[26] = jnp.ones((LEVELS, LANES), F32)
    for copy in copies:
        copy.wait()
    even = lax.rem(lax.axis_index("lat"), 2) == 0
    side_a = jnp.where(even, 1, 0)
    row_a = jnp.where(even, HALO, 0)
    side_b = jnp.where(even, 0, 1)
    row_b = jnp.where(even, 0, HALO - 1)
    for out, side, row, count, flat in ((out_a, side_a, row_a, HALO, 0), (out_b, side_b, row_b, HALO + 1, 1)):
        cut = [ref.at[side].reshape(LEVELS * 8, LANES) for ref in rims[:6]]
        for i in range(count):
            for f, value in enumerate(own_row(cut, row + i)):
                out[5 * i + f] = value
            for f in range(2):
                place = (20, HALO * f + i) if flat == 0 else (25 + f, i)
                out[place[0], pl.ds(place[1], 1), :] = rims[6 + f][side, pl.ds(row + i, 1), :]


def halo_rows(got_a, got_b):
    even = lax.rem(lax.axis_index("lat"), 2) == 0

    def spread(row):
        return jnp.broadcast_to(row, (LEVELS, LANES))

    def read_a(i, f):
        if f < 5:
            return got_a[5 * i + f]
        return spread(got_a[20, pl.ds(HALO * (f - 5) + i, 1), :])

    def read_b(i, f):
        if f < 5:
            return got_b[5 * i + f]
        return spread(got_b[20 + f, pl.ds(i, 1), :])

    def sane(value, f):
        return value if f < 5 else jnp.where(value > 0.0, value, 1.0)

    def south(i, f):
        return sane(jnp.where(even, read_b(i + 1, f), read_a(i, f)), f)

    def north(i, f):
        return sane(jnp.where(even, read_a(i, f), read_b(i, f)), f)

    def fold(i, f):
        return sane(read_b(i, f), f)

    return south, north, fold


def interior_kernel(*refs):
    ins = refs[:8]
    state_out, own, msgs, rims = refs[8:12]
    state = [state_out.at[f] for f in range(4)]
    geo = dict(zip(GEO, refs[12:22]))
    blank = jnp.zeros((LEVELS, LANES), F32)
    for ref in state + [geo["half"]]:
        ref[0] = blank
        ref[ROWS + 1] = blank

    def take(row, carry):
        values = own_row(ins, row)
        for ref, value in zip(state, values):
            ref[row + 1] = value
        geo["half"][row + 1] = values[4]
        return carry

    lax.fori_loop(0, ROWS, take, 0, unroll=8)
    for i in range(8):
        for place, row in ((i, i), (8 + i, ROWS - 8 + i)):
            for f in range(4):
                rims[f, place] = state[f][row + 1]
            rims[4, place] = geo["half"][row + 1]
            rims[5, place] = wide(ins[6], row)
            rims[6, place] = wide(ins[7], row)

    lane = lanes()
    part = (lane // HALO) % (GROUP // HALO)

    def pack(g, carry):
        packs = []
        for f in range(7):
            west = east = jnp.zeros((LEVELS, LANES), F32)
            for q in range(8):
                row = jnp.clip(BLOCK * q + g - HALO, 0, ROWS - 1)
                if f < 4:
                    value = state[f][row + 1]
                elif f == 4:
                    value = geo["half"][row + 1]
                else:
                    value = wide(ins[f + 1], row)
                here = (lane // GROUP) == q
                west = jnp.where(here, roll(value, GROUP * q + HALO), west)
                east = jnp.where(here, roll(value, GROUP * q + 12), east)
            own[0, f, g] = west
            own[1, f, g] = east
            packs.append((west, east))
        for side in range(2):
            for half, first in ((0, 0), (1, 4)):
                message = jnp.zeros((LEVELS, LANES), F32)
                for f in range(4 if half == 0 else 3):
                    value = packs[first + f][side]
                    shift = HALO * f - (HALO if side == 0 else 2 * HALO)
                    message = jnp.where(part == f, roll(value, shift), message)
                msgs[side, BLOCK * half + g] = message
        return carry

    lax.fori_loop(0, BLOCK, pack, 0)

    def shape(row, carry):
        geometry_row(geo, row + 1, wide(ins[6], row), wide(ins[7], row), wide(ins[6], row + 1), wide(ins[7], row + 1))
        return carry

    lax.fori_loop(0, ROWS - 1, shape, 0, unroll=7)

    def step(s, carry):
        last = s == NSTEP
        march(state, geo, ((jnp.where(last, 1 + HALO, 1), jnp.where(last, ROWS - 2 * HALO, ROWS)),), 8)
        return carry

    lax.fori_loop(1, NSTEP + 1, step, 0)


def columns_kernel(msgs, got_a, got_b, out_a, out_b):
    even = lax.rem(lax.axis_index("lon"), 2) == 0
    top = lax.axis_index("lat") == lax.axis_size("lat") - 1
    south, north, fold = halo_rows(got_a, got_b)
    lane = lanes()
    part = (lane // HALO) % (GROUP // HALO)
    for half, first in ((0, 0), (1, 4)):
        for g in range(BLOCK):
            slot = BLOCK * half + g
            west, east = msgs[0, slot], msgs[1, slot]
            if g != HALO:
                add_w = add_e = jnp.zeros((LEVELS, LANES), F32)
                base = 0 if g < HALO else 7 * GROUP
                for f in range(4 if half == 0 else 3):
                    if g < HALO:
                        value = south(g, first + f)
                    else:
                        value = jnp.where(top, fold(g - 4, first + f), north(g - 5, first + f))
                    add_w = jnp.where(part == f, roll(value, base + HALO * f), add_w)
                    add_e = jnp.where(part == f, roll(value, base + HALO * f + HALO), add_e)
                if g < HALO:
                    here = lane < GROUP
                else:
                    here = lane >= 7 * GROUP
                    add_w, add_e = jnp.where(top, add_e, add_w), jnp.where(top, add_w, add_e)
                west = jnp.where(here, add_w, west)
                east = jnp.where(here, add_e, east)
            out_a[slot] = jnp.where(even, east, west)
            out_b[slot] = jnp.where(even, west, east)


SOUTH, NORTH, FOLD, NS_ROWS = 0, 12, 24, 30


def rows_strip_kernel(*refs):
    rims, got_a, got_b, hinge, out = refs[:5]
    state = refs[5:9]
    east_w, north_w = refs[9:11]
    geo = dict(zip(GEO, refs[11:]))
    top = lax.axis_index("lat") == lax.axis_size("lat") - 1
    pivot = hinge[0]
    south, north, fold = halo_rows(got_a, got_b)
    fields = list(state) + [geo["half"], east_w, north_w]
    for f, ref in enumerate(fields):
        for i in range(HALO):
            ref[SOUTH + i] = south(i, f)
            ref[NORTH + 8 + i] = north(i, f)
            ref[FOLD + i] = fold(i, f)
        ref[FOLD + HALO] = fold(HALO, f)
        for i in range(8):
            ref[SOUTH + HALO + i] = rims[f, i]
            ref[NORTH + i] = rims[f, 8 + i]

    def refold(ref, sign):
        ghost = sign * mirrored(ref[FOLD + 4 - pivot], LANES)
        ref[FOLD + 5] = sign * mirrored(ref[NORTH + 7 - pivot], LANES)
        ref[NORTH + 8] = jnp.where(top, ghost, ref[NORTH + 8])

    for ref in fields[4:]:
        refold(ref, 1.0)
    for row in (*range(SOUTH, SOUTH + 11), *range(NORTH, NORTH + 11), *range(FOLD, FOLD + 5)):
        geometry_row(geo, row, east_w[row], north_w[row], east_w[row + 1], north_w[row + 1])

    for s in range(1, NSTEP + 1):
        for ref, sign in zip(state, SIGNS):
            refold(ref, sign)
        chains = [(SOUTH + s, 12 - 2 * s), (NORTH + s, 12 - 2 * s)]
        if s < NSTEP:
            chains.append((FOLD + s, 5 - s))
        march(state, geo, chains)

    for f, ref in enumerate(state):
        for i in range(HALO):
            out[f, i] = ref[SOUTH + HALO + i]
            out[f, HALO + i] = ref[NORTH + HALO + i]


WEST, EAST, FOLDS, WE_ROWS = 0, 11, 22, 28


def columns_strip_kernel(*refs):
    own, lon_a, lon_b, got_a, got_b, inner, strips, hinge = refs[:8]
    outs = refs[8:13]
    state = refs[13:17]
    east_w, north_w = refs[17:19]
    geo = dict(zip(GEO, refs[19:]))
    even = lax.rem(lax.axis_index("lon"), 2) == 0
    top = lax.axis_index("lat") == lax.axis_size("lat") - 1
    pivot = hinge[0]
    south, north, fold = halo_rows(got_a, got_b)
    fields = list(state) + [geo["half"], east_w, north_w]
    lane = lanes()
    inside = lane % GROUP

    def message(side, f, g):
        slot = g if f < 4 else BLOCK + g
        a, b = lon_a[slot], lon_b[slot]
        return jnp.where(even, b, a) if side == 0 else jnp.where(even, a, b)

    for g in range(BLOCK):
        for f, ref in enumerate(fields):
            west, east = own[0, f, g], own[1, f, g]
            if g < HALO:
                value = south(g, f)
                west = jnp.where(lane < GROUP, roll(value, HALO), west)
                east = jnp.where(lane < GROUP, roll(value, 12), east)
            elif g > HALO:
                value = north(g - 5, f)
                west = jnp.where(lane >= 7 * GROUP, roll(value, 7 * GROUP + HALO), west)
                east = jnp.where(lane >= 7 * GROUP, roll(value, 7 * GROUP + 12), east)
            shift = -HALO * (f % 4)
            west = jnp.where(inside < HALO, roll(message(0, f, g), shift), west)
            east = jnp.where(inside >= 12, roll(message(1, f, g), shift + 12), east)
            if f > 4:
                west = jnp.where(west > 0.0, west, 1.0)
                east = jnp.where(east > 0.0, east, 1.0)
            ref[WEST + 1 + g] = west
            ref[EAST + 1 + g] = east

    def rewrap(ref):
        for base in (WEST, EAST):
            ref[base] = roll(ref[base + 9], GROUP)
            ref[base + 10] = roll(ref[base + 1], -GROUP)

    def refold(ref, sign):
        ghost = sign * mirrored(ref[FOLDS + 4 - pivot], GROUP)
        from_e, from_w = ref[EAST + 5 - pivot], ref[WEST + 5 - pivot]
        back = jnp.where(lane < GROUP, roll(from_e, GROUP), roll(from_w, 2 * GROUP))
        ref[FOLDS + 5] = sign * mirrored(back, GROUP)
        here = (lane >= 7 * GROUP) & top
        ref[WEST + 6] = jnp.where(here, roll(ghost, 6 * GROUP), ref[WEST + 6])
        ref[EAST + 6] = jnp.where(here, roll(ghost, 7 * GROUP), ref[EAST + 6])

    for i in range(HALO + 1):
        for f, ref in enumerate(fields):
            value = fold(i, f)
            value = jnp.where(lane < GROUP, roll(value, HALO), roll(value, 28))
            if i > 0:
                slot = HALO + i
                corner = 7 * GROUP + HALO * (f % 4)
                value = jnp.where(lane < HALO, roll(message(1, f, slot), -corner), value)
                other = roll(message(0, f, slot), 28 - corner)
                value = jnp.where((lane >= 28) & (lane < 32), other, value)
            if f > 4:
                value = jnp.where(value > 0.0, value, 1.0)
            ref[FOLDS + i] = value
    for ref in fields[4:]:
        refold(ref, 1.0)
        rewrap(ref)
    for row in (*range(WEST, WEST + 10), *range(EAST, EAST + 10), *range(FOLDS, FOLDS + 5)):
        geometry_row(geo, row, east_w[row], north_w[row], east_w[row + 1], north_w[row + 1])

    def step(s, carry):
        for ref, sign in zip(state, SIGNS):
            refold(ref, sign)
            rewrap(ref)
        march(state, geo, ((WEST + 1, BLOCK), (EAST + 1, BLOCK), (FOLDS + 1, 4)))
        return carry

    lax.fori_loop(1, NSTEP + 1, step, 0)

    for ref in state:
        for g in range(BLOCK):
            ref[WEST + 1 + g] = jnp.where(inside < HALO, roll(ref[EAST + 1 + g], -8), ref[WEST + 1 + g])
    rim = (lane < HALO) | (lane >= LANES - HALO)
    terms = eos_terms()

    def emit(row, bases, q, g):
        new = [
            jnp.where(rim, roll(ref[WEST + 1 + g], -(GROUP * q + HALO)), base) for ref, base in zip(state, bases)
        ]
        new.append(density_of(new[0], new[1], terms))
        for ref, value in zip(outs, new):
            ref[pl.ds(row, LEVELS, stride=ROWS), :] = value

    for i in range(HALO):
        emit(i, [strips[f, i] for f in range(4)], 0, HALO + i)
        emit(ROWS - HALO + i, [strips[f, HALO + i] for f in range(4)], 7, 1 + i)
    emit(HALO, [inner[f, HALO + 1] for f in range(4)], 0, 8)
    emit(ROWS - HALO - 1, [inner[f, ROWS - HALO] for f in range(4)], 7, 0)

    def merge(g, carry):
        for q in range(1, 7):
            row = BLOCK * q + g - HALO
            emit(row, [inner[f, row + 1] for f in range(4)], q, g)
        return carry

    lax.fori_loop(0, BLOCK, merge, 0)


def call(kernel, ins, outs, scratch=(), smem_last=False, far=False, flops=0, limit=40):
    specs = [pl.BlockSpec(memory_space=pltpu.HBM if far else pltpu.VMEM) for _ in ins]
    if smem_last:
        specs[-1] = pl.BlockSpec(memory_space=pltpu.SMEM)
    return pl.pallas_call(
        kernel,
        out_shape=[jax.ShapeDtypeStruct(shape, F32) for shape in outs],
        in_specs=specs,
        out_specs=[pl.BlockSpec(memory_space=pltpu.VMEM) for _ in outs],
        scratch_shapes=list(scratch),
        compiler_params=pltpu.CompilerParams(vmem_limit_bytes=limit * MIB),
        cost_estimate=pl.CostEstimate(flops=flops, bytes_accessed=2_000_000, transcendentals=0),
    )(*ins)


def lat_pairs(lat, lon):
    first = [(a * lon + o, (a ^ 1) * lon + o) for a in range(lat) for o in range(lon)]
    second = [
        (a * lon + o, (a + 1 if a % 2 else a - 1) * lon + o) for a in range(1, lat - 1) for o in range(lon)
    ]
    second += [((lat - 1) * lon + o, (lat - 1) * lon + lon - 1 - o) for o in range(lon)]
    return first, second


def lon_pairs(lat, lon):
    first = [(a * lon + o, a * lon + (o ^ 1)) for a in range(lat) for o in range(lon)]
    second = [
        (a * lon + o, a * lon + ((o + 1) if o % 2 else (o - 1)) % lon) for a in range(lat) for o in range(lon)
    ]
    return first, second


def on_device(*args):
    lat, lon = lax.axis_size("lat"), lax.axis_size("lon")
    axes = ("lat", "lon")
    hinge = args[8]
    tile = (LEVELS, LANES)
    fields = [*args[:4], args[6], args[7], args[4], args[5]]
    flat = [x.reshape(LEVELS * ROWS, LANES) for x in fields[:6]] + fields[6:]
    kinds = [F32] * 5 + [jnp.int32] + [F32] * 2
    state_scratch = lambda rows: [pltpu.VMEM((rows,) + tile, F32) for _ in range(6)]

    rows_a, rows_b = call(
        rows_kernel,
        fields,
        [(21,) + tile, (27,) + tile],
        [pltpu.VMEM((2, LEVELS) + tile, kind) for kind in kinds[:6]]
        + [pltpu.VMEM((2,) + tile, F32)] * 2
        + [pltpu.SemaphoreType.DMA((8, 2))],
        far=True,
        limit=54,
    )
    pairs_a, pairs_b = lat_pairs(lat, lon)
    got_b = lax.ppermute(rows_b, axes, pairs_b)
    got_a = lax.ppermute(rows_a, axes, pairs_a)
    inner, own, msgs, rims = call(
        interior_kernel,
        flat,
        [(4, ROWS + 2) + tile, (2, 7, BLOCK) + tile, (2, 2 * BLOCK) + tile, (7, 16) + tile],
        geo_scratch(ROWS + 2),
        flops=40_000_000,
        limit=50,
    )
    cols_a, cols_b = call(columns_kernel, [msgs, got_a, got_b], [(2 * BLOCK,) + tile] * 2)
    pairs_a, pairs_b = lon_pairs(lat, lon)
    lon_b = lax.ppermute(cols_b, axes, pairs_b)
    lon_a = lax.ppermute(cols_a, axes, pairs_a)
    (strips,) = call(
        rows_strip_kernel,
        [rims, got_a, got_b, hinge],
        [(4, 2 * HALO) + tile],
        state_scratch(NS_ROWS) + geo_scratch(NS_ROWS),
        smem_last=True,
        flops=10_000_000,
    )
    outs = call(
        columns_strip_kernel,
        [own, lon_a, lon_b, got_a, got_b, inner, strips, hinge],
        [(LEVELS * ROWS, LANES)] * 5,
        state_scratch(WE_ROWS) + geo_scratch(WE_ROWS),
        smem_last=True,
        flops=10_000_000,
    )
    return tuple(x.reshape(LEVELS, ROWS, LANES) for x in outs)


def solution(mesh):
    field = P(None, "lat", "lon")
    flat = P("lat", "lon")
    return jax.shard_map(
        on_device,
        mesh=mesh,
        in_specs=(field, field, field, field, flat, flat, field, field, P()),
        out_specs=(field,) * 5,
        check_vma=False,
    )
```

```python
import jax
import jax.numpy as jnp
from jax import lax
from jax.experimental import pallas as pl
from jax.experimental.pallas import tpu as pltpu
from jax.sharding import PartitionSpec as P

F32 = jnp.float32
NSTEP = 4
LEVELS = 8
ROWS = 64
LANES = 128
HALO = 4
BLOCK = 9
GROUP = 16

time_step = 0.2
diffusivity = 0.4
eos_alpha = 0.1655
eos_beta = 0.76554
eos_lambda_one = 0.05952
eos_lambda_two = 0.00054914
eos_mu_one = 0.0001497
eos_mu_two = 1.109e-05
eos_cross = 0.0024341

SIGNS = (1.0, 1.0, -1.0, -1.0)
MIB = 1024 * 1024


def roll(x, shift):
    shift = shift % LANES
    return pltpu.roll(x, shift, 1) if shift else x


def lanes():
    return lax.broadcasted_iota(jnp.int32, (LEVELS, LANES), 1)


def levels():
    return lax.broadcasted_iota(jnp.int32, (LEVELS, LANES), 0)


def mirrored(x, width):
    lane = lanes()
    bit = 1
    while bit < width:
        x = jnp.where((lane & bit) != 0, roll(x, bit), roll(x, -bit))
        bit *= 2
    return x


def eos_terms():
    depth = 100.0 * (levels().astype(F32) + 0.5)
    return -eos_alpha * (1.0 + eos_mu_one * depth), eos_beta * (1.0 - eos_mu_two * depth)


def density_of(heat, salt, terms):
    heat_term, salt_term = terms
    return heat * (heat_term - (0.5 * eos_alpha * eos_lambda_one) * heat - eos_cross * salt) + salt * (
        salt_term - (0.5 * eos_beta * eos_lambda_two) * salt
    )


def pressure_of(heat, salt, half_depth, terms):
    half = density_of(heat, salt, terms) * half_depth
    level = levels()
    total = half
    for shift in (1, 2, 4):
        total = total + jnp.where(level >= shift, pltpu.roll(total, shift, 0), 0.0)
    return total + total - half


def geometry_row(geo, row, east0, north0, east1, north1):
    half0 = geo["half"][row]
    half1 = geo["half"][row + 1]
    half_e = roll(half0, -1)
    span = 2.0 / (east0 + roll(east0, -1))
    side = 0.5 * (north0 + roll(north0, -1))
    open_e = jnp.minimum(half0, half_e) > 0.0
    area = jnp.where(open_e, side * (half0 + half_e), 0.0)
    geo["area_e"][row] = area
    geo["cond_e"][row] = diffusivity * area * span
    geo["open_e"][row] = jnp.where(open_e, 1.0, 0.0)
    geo["push_e"][row] = time_step * span
    span = 2.0 / (north0 + north1)
    side = 0.5 * (east0 + east1)
    open_n = jnp.minimum(half0, half1) > 0.0
    area = jnp.where(open_n, side * (half0 + half1), 0.0)
    geo["area_n"][row] = area
    geo["cond_n"][row] = diffusivity * area * span
    geo["open_n"][row] = jnp.where(open_n, 1.0, 0.0)
    geo["push_n"][row] = time_step * span
    geo["inv"][row] = (0.5 * time_step) / (east0 * north0 * jnp.where(half0 > 0.0, half0, 1.0))


def march(state, geo, chains):
    terms = eos_terms()

    def north_face(row, speed):
        flow = geo["area_n"][row] * speed
        ahead = jnp.maximum(flow, 0.0) + geo["cond_n"][row]
        return ahead, flow - ahead

    def begin(row):
        before = tuple(ref[row - 1] for ref in state)
        here = tuple(ref[row] for ref in state)
        return before + here + north_face(row - 1, before[3]) + (pressure_of(here[0], here[1], geo["half"][row], terms),)

    def advance(row, carry):
        before, here = carry[0:4], carry[4:8]
        south_p, south_m, press = carry[8:]
        north = tuple(ref[row + 1] for ref in state)
        press_n = pressure_of(north[0], north[1], geo["half"][row + 1], terms)
        north_p, north_m = north_face(row, here[3])
        flow = geo["area_e"][row] * here[2]
        east_p = jnp.maximum(flow, 0.0) + geo["cond_e"][row]
        east_m = flow - east_p
        west_p, west_m = roll(east_p, 1), roll(east_m, 1)
        inv = geo["inv"][row]
        keep = 1.0 - inv * ((east_p - west_m) + (north_p - south_m))
        c_e, c_w, c_n, c_s = inv * east_m, inv * west_p, inv * north_m, inv * south_p
        new = [
            keep * c + (c_w * roll(c, 1) + c_s * s) - (c_e * roll(c, -1) + c_n * n)
            for c, s, n in zip(here, before, north)
        ]
        new[2] = (new[2] + (press - roll(press, -1)) * geo["push_e"][row]) * geo["open_e"][row]
        new[3] = (new[3] + (press - press_n) * geo["push_n"][row]) * geo["open_n"][row]
        for ref, value in zip(state, new):
            ref[row] = value
        return here + north + (north_p, north_m, press_n)

    carries = [begin(first) for first, _ in chains]
    for u in range(max(count for _, count in chains)):
        for index, (first, count) in enumerate(chains):
            if u < count:
                carries[index] = advance(first + u, carries[index])


GEO = ("half", "area_e", "cond_e", "open_e", "push_e", "area_n", "cond_n", "open_n", "push_n", "inv")


def geo_scratch(rows):
    return [pltpu.VMEM((rows, LEVELS, LANES), F32) for _ in GEO]


def column_of(ref, row):
    return ref[pl.ds(row, LEVELS, stride=ref.shape[0] // LEVELS), :]


def wide(ref, row):
    return jnp.broadcast_to(ref[pl.ds(row, 1), :], (LEVELS, LANES))


def own_row(refs, row):
    heat, salt, east, north, thick, water = [column_of(ref, row) for ref in refs[:6]]
    wet = water.astype(F32)
    return heat * wet, salt * wet, east, north, 0.5 * (thick * wet)


def rows_kernel(*refs):
    ins, (out_a, out_b) = refs[:8], refs[8:10]
    rims, sems = refs[10:18], refs[18]
    copies = []
    for f, (src, dst) in enumerate(zip(ins, rims)):
        for side, row in ((0, 0), (1, ROWS - 8)):
            if f < 6:
                pair = src.at[:, pl.ds(row, 8), :], dst.at[side]
            else:
                pair = src.at[pl.ds(row, 8), :], dst.at[side]
            copies.append(pltpu.make_async_copy(*pair, sems.at[f, side]))
    for copy in copies:
        copy.start()
    out_b[25] = jnp.ones((LEVELS, LANES), F32)
    out_b[26] = jnp.ones((LEVELS, LANES), F32)
    for copy in copies:
        copy.wait()
    even = lax.rem(lax.axis_index("lat"), 2) == 0
    side_a = jnp.where(even, 1, 0)
    row_a = jnp.where(even, HALO, 0)
    side_b = jnp.where(even, 0, 1)
    row_b = jnp.where(even, 0, HALO - 1)
    for out, side, row, count, flat in ((out_a, side_a, row_a, HALO, 0), (out_b, side_b, row_b, HALO + 1, 1)):
        cut = [ref.at[side].reshape(LEVELS * 8, LANES) for ref in rims[:6]]
        for i in range(count):
            for f, value in enumerate(own_row(cut, row + i)):
                out[5 * i + f] = value
            for f in range(2):
                place = (20, HALO * f + i) if flat == 0 else (25 + f, i)
                out[place[0], pl.ds(place[1], 1), :] = rims[6 + f][side, pl.ds(row + i, 1), :]


def halo_rows(got_a, got_b):
    even = lax.rem(lax.axis_index("lat"), 2) == 0

    def spread(row):
        return jnp.broadcast_to(row, (LEVELS, LANES))

    def read_a(i, f):
        if f < 5:
            return got_a[5 * i + f]
        return spread(got_a[20, pl.ds(HALO * (f - 5) + i, 1), :])

    def read_b(i, f):
        if f < 5:
            return got_b[5 * i + f]
        return spread(got_b[20 + f, pl.ds(i, 1), :])

    def sane(value, f):
        return value if f < 5 else jnp.where(value > 0.0, value, 1.0)

    def south(i, f):
        return sane(jnp.where(even, read_b(i + 1, f), read_a(i, f)), f)

    def north(i, f):
        return sane(jnp.where(even, read_a(i, f), read_b(i, f)), f)

    def fold(i, f):
        return sane(read_b(i, f), f)

    return south, north, fold


def interior_kernel(*refs):
    ins = refs[:8]
    state_out, own, msgs, rims = refs[8:12]
    state = [state_out.at[f] for f in range(4)]
    geo = dict(zip(GEO, refs[12:22]))
    blank = jnp.zeros((LEVELS, LANES), F32)
    for ref in state + [geo["half"]]:
        ref[0] = blank
        ref[ROWS + 1] = blank

    def take(row, carry):
        values = own_row(ins, row)
        for ref, value in zip(state, values):
            ref[row + 1] = value
        geo["half"][row + 1] = values[4]
        return carry

    lax.fori_loop(0, ROWS, take, 0, unroll=8)
    for i in range(8):
        for place, row in ((i, i), (8 + i, ROWS - 8 + i)):
            for f in range(4):
                rims[f, place] = state[f][row + 1]
            rims[4, place] = geo["half"][row + 1]
            rims[5, place] = wide(ins[6], row)
            rims[6, place] = wide(ins[7], row)

    lane = lanes()
    part = (lane // HALO) % (GROUP // HALO)

    def pack(g, carry):
        packs = []
        for f in range(7):
            west = east = jnp.zeros((LEVELS, LANES), F32)
            for q in range(8):
                row = jnp.clip(BLOCK * q + g - HALO, 0, ROWS - 1)
                if f < 4:
                    value = state[f][row + 1]
                elif f == 4:
                    value = geo["half"][row + 1]
                else:
                    value = wide(ins[f + 1], row)
                here = (lane // GROUP) == q
                west = jnp.where(here, roll(value, GROUP * q + HALO), west)
                east = jnp.where(here, roll(value, GROUP * q + 12), east)
            own[0, f, g] = west
            own[1, f, g] = east
            packs.append((west, east))
        for side in range(2):
            for half, first in ((0, 0), (1, 4)):
                message = jnp.zeros((LEVELS, LANES), F32)
                for f in range(4 if half == 0 else 3):
                    value = packs[first + f][side]
                    shift = HALO * f - (HALO if side == 0 else 2 * HALO)
                    message = jnp.where(part == f, roll(value, shift), message)
                msgs[side, BLOCK * half + g] = message
        return carry

    lax.fori_loop(0, BLOCK, pack, 0, unroll=3)

    def shape(row, carry):
        geometry_row(geo, row + 1, wide(ins[6], row), wide(ins[7], row), wide(ins[6], row + 1), wide(ins[7], row + 1))
        return carry

    lax.fori_loop(0, ROWS - 1, shape, 0, unroll=7)

    def step(s, carry):
        march(state, geo, ((2, ROWS - 2),))
        return carry

    lax.fori_loop(1, NSTEP + 1, step, 0)


def columns_kernel(msgs, got_a, got_b, out_a, out_b):
    even = lax.rem(lax.axis_index("lon"), 2) == 0
    top = lax.axis_index("lat") == lax.axis_size("lat") - 1
    south, north, fold = halo_rows(got_a, got_b)
    lane = lanes()
    part = (lane // HALO) % (GROUP // HALO)
    for half, first in ((0, 0), (1, 4)):
        for g in range(BLOCK):
            slot = BLOCK * half + g
            west, east = msgs[0, slot], msgs[1, slot]
            if g != HALO:
                add_w = add_e = jnp.zeros((LEVELS, LANES), F32)
                base = 0 if g < HALO else 7 * GROUP
                for f in range(4 if half == 0 else 3):
                    if g < HALO:
                        value = south(g, first + f)
                    else:
                        value = jnp.where(top, fold(g - 4, first + f), north(g - 5, first + f))
                    add_w = jnp.where(part == f, roll(value, base + HALO * f), add_w)
                    add_e = jnp.where(part == f, roll(value, base + HALO * f + HALO), add_e)
                if g < HALO:
                    here = lane < GROUP
                else:
                    here = lane >= 7 * GROUP
                    add_w, add_e = jnp.where(top, add_e, add_w), jnp.where(top, add_w, add_e)
                west = jnp.where(here, add_w, west)
                east = jnp.where(here, add_e, east)
            out_a[slot] = jnp.where(even, east, west)
            out_b[slot] = jnp.where(even, west, east)


SOUTH, NORTH, FOLD, NS_ROWS = 0, 12, 24, 30


def rows_strip_kernel(*refs):
    rims, got_a, got_b, hinge, out = refs[:5]
    state = refs[5:9]
    east_w, north_w = refs[9:11]
    geo = dict(zip(GEO, refs[11:]))
    top = lax.axis_index("lat") == lax.axis_size("lat") - 1
    pivot = hinge[0]
    south, north, fold = halo_rows(got_a, got_b)
    fields = list(state) + [geo["half"], east_w, north_w]
    for f, ref in enumerate(fields):
        for i in range(HALO):
            ref[SOUTH + i] = south(i, f)
            ref[NORTH + 8 + i] = north(i, f)
            ref[FOLD + i] = fold(i, f)
        ref[FOLD + HALO] = fold(HALO, f)
        for i in range(8):
            ref[SOUTH + HALO + i] = rims[f, i]
            ref[NORTH + i] = rims[f, 8 + i]

    def refold(ref, sign):
        ghost = sign * mirrored(ref[FOLD + 4 - pivot], LANES)
        ref[FOLD + 5] = sign * mirrored(ref[NORTH + 7 - pivot], LANES)
        ref[NORTH + 8] = jnp.where(top, ghost, ref[NORTH + 8])

    for ref in fields[4:]:
        refold(ref, 1.0)
    for row in (*range(SOUTH, SOUTH + 11), *range(NORTH, NORTH + 11), *range(FOLD, FOLD + 5)):
        geometry_row(geo, row, east_w[row], north_w[row], east_w[row + 1], north_w[row + 1])

    for s in range(1, NSTEP + 1):
        for ref, sign in zip(state, SIGNS):
            refold(ref, sign)
        chains = [(SOUTH + s, 12 - 2 * s), (NORTH + s, 12 - 2 * s)]
        if s < NSTEP:
            chains.append((FOLD + s, 5 - s))
        march(state, geo, chains)

    for f, ref in enumerate(state):
        for i in range(HALO):
            out[f, i] = ref[SOUTH + HALO + i]
            out[f, HALO + i] = ref[NORTH + HALO + i]


WEST, EAST, FOLDS, WE_ROWS = 0, 11, 22, 28


def columns_strip_kernel(*refs):
    own, lon_a, lon_b, got_a, got_b, inner, strips, hinge = refs[:8]
    outs = refs[8:13]
    state = refs[13:17]
    east_w, north_w = refs[17:19]
    geo = dict(zip(GEO, refs[19:29]))
    stage, sems = refs[29:34], refs[34]
    even = lax.rem(lax.axis_index("lon"), 2) == 0
    top = lax.axis_index("lat") == lax.axis_size("lat") - 1
    below = hinge[0] == 1
    south, north, fold = halo_rows(got_a, got_b)
    fields = list(state) + [geo["half"], east_w, north_w]
    lane = lanes()
    inside = lane % GROUP

    def message(side, f, g):
        slot = g if f < 4 else BLOCK + g
        a, b = lon_a[slot], lon_b[slot]
        return jnp.where(even, b, a) if side == 0 else jnp.where(even, a, b)

    for g in range(BLOCK):
        for f, ref in enumerate(fields):
            west, east = own[0, f, g], own[1, f, g]
            if g < HALO:
                value = south(g, f)
                west = jnp.where(lane < GROUP, roll(value, HALO), west)
                east = jnp.where(lane < GROUP, roll(value, 12), east)
            elif g > HALO:
                value = north(g - 5, f)
                west = jnp.where(lane >= 7 * GROUP, roll(value, 7 * GROUP + HALO), west)
                east = jnp.where(lane >= 7 * GROUP, roll(value, 7 * GROUP + 12), east)
            shift = -HALO * (f % 4)
            west = jnp.where(inside < HALO, roll(message(0, f, g), shift), west)
            east = jnp.where(inside >= 12, roll(message(1, f, g), shift + 12), east)
            if f > 4:
                west = jnp.where(west > 0.0, west, 1.0)
                east = jnp.where(east > 0.0, east, 1.0)
            ref[WEST + 1 + g] = west
            ref[EAST + 1 + g] = east

    def rewrap(ref):
        for base in (WEST, EAST):
            ref[base] = roll(ref[base + 9], GROUP)
            ref[base + 10] = roll(ref[base + 1], -GROUP)

    def refold(ref, sign):
        ghost = sign * mirrored(jnp.where(below, ref[FOLDS + 3], ref[FOLDS + 4]), GROUP)
        from_e = jnp.where(below, ref[EAST + 4], ref[EAST + 5])
        from_w = jnp.where(below, ref[WEST + 4], ref[WEST + 5])
        back = jnp.where(lane < GROUP, roll(from_e, GROUP), roll(from_w, 2 * GROUP))
        ref[FOLDS + 5] = sign * mirrored(back, GROUP)
        here = (lane >= 7 * GROUP) & top
        ref[WEST + 6] = jnp.where(here, roll(ghost, 6 * GROUP), ref[WEST + 6])
        ref[EAST + 6] = jnp.where(here, roll(ghost, 7 * GROUP), ref[EAST + 6])

    for i in range(HALO + 1):
        for f, ref in enumerate(fields):
            value = fold(i, f)
            value = jnp.where(lane < GROUP, roll(value, HALO), roll(value, 28))
            if i > 0:
                slot = HALO + i
                corner = 7 * GROUP + HALO * (f % 4)
                value = jnp.where(lane < HALO, roll(message(1, f, slot), -corner), value)
                other = roll(message(0, f, slot), 28 - corner)
                value = jnp.where((lane >= 28) & (lane < 32), other, value)
            if f > 4:
                value = jnp.where(value > 0.0, value, 1.0)
            ref[FOLDS + i] = value
    for ref in fields[4:]:
        refold(ref, 1.0)
        rewrap(ref)
    for row in (*range(WEST, WEST + 10), *range(EAST, EAST + 10), *range(FOLDS, FOLDS + 5)):
        geometry_row(geo, row, east_w[row], north_w[row], east_w[row + 1], north_w[row + 1])

    def step(s, carry):
        for ref, sign in zip(state, SIGNS):
            refold(ref, sign)
            rewrap(ref)
        march(state, geo, ((WEST + 1, BLOCK), (EAST + 1, BLOCK), (FOLDS + 1, 4)))
        return carry

    lax.fori_loop(1, NSTEP + 1, step, 0)

    for ref in state:
        for g in range(BLOCK):
            ref[WEST + 1 + g] = jnp.where(inside < HALO, roll(ref[EAST + 1 + g], -8), ref[WEST + 1 + g])
    rim = (lane < HALO) | (lane >= LANES - HALO)
    terms = eos_terms()

    copies = []
    for row in range(ROWS):
        q, g = divmod(row + HALO, BLOCK)
        if HALO <= row < ROWS - HALO:
            bases = [inner[f, row + 1] for f in range(4)]
        else:
            place = row if row < HALO else row - (ROWS - 2 * HALO)
            bases = [strips[f, place] for f in range(4)]
        new = [
            jnp.where(rim, roll(ref[WEST + 1 + g], -(GROUP * q + HALO)), base) for ref, base in zip(state, bases)
        ]
        new.append(density_of(new[0], new[1], terms))
        for ref, value in zip(stage, new):
            ref.reshape(LEVELS * ROWS, LANES)[pl.ds(row, LEVELS, stride=ROWS), :] = value
        if row % 8 == 7:
            rows = pl.ds(row - 7, 8)
            for f in range(5):
                copy = pltpu.make_async_copy(stage[f].at[:, rows, :], outs[f].at[:, rows, :], sems.at[f, row // 8])
                copy.start()
                copies.append(copy)
    for copy in copies:
        copy.wait()


def call(kernel, ins, outs, scratch=(), smem_last=False, far=False, out_far=False, flops=0, limit=40):
    specs = [pl.BlockSpec(memory_space=pltpu.HBM if far else pltpu.VMEM) for _ in ins]
    if smem_last:
        specs[-1] = pl.BlockSpec(memory_space=pltpu.SMEM)
    return pl.pallas_call(
        kernel,
        out_shape=[jax.ShapeDtypeStruct(shape, F32) for shape in outs],
        in_specs=specs,
        out_specs=[pl.BlockSpec(memory_space=pltpu.HBM if out_far else pltpu.VMEM) for _ in outs],
        scratch_shapes=list(scratch),
        compiler_params=pltpu.CompilerParams(vmem_limit_bytes=limit * MIB),
        cost_estimate=pl.CostEstimate(flops=flops, bytes_accessed=2_000_000, transcendentals=0),
    )(*ins)


def lat_pairs(lat, lon):
    first = [(a * lon + o, (a ^ 1) * lon + o) for a in range(lat) for o in range(lon)]
    second = [
        (a * lon + o, (a + 1 if a % 2 else a - 1) * lon + o) for a in range(1, lat - 1) for o in range(lon)
    ]
    second += [((lat - 1) * lon + o, (lat - 1) * lon + lon - 1 - o) for o in range(lon)]
    return first, second


def lon_pairs(lat, lon):
    first = [(a * lon + o, a * lon + (o ^ 1)) for a in range(lat) for o in range(lon)]
    second = [
        (a * lon + o, a * lon + ((o + 1) if o % 2 else (o - 1)) % lon) for a in range(lat) for o in range(lon)
    ]
    return first, second


def on_device(*args):
    lat, lon = lax.axis_size("lat"), lax.axis_size("lon")
    axes = ("lat", "lon")
    hinge = args[8]
    tile = (LEVELS, LANES)
    fields = [*args[:4], args[6], args[7], args[4], args[5]]
    flat = [x.reshape(LEVELS * ROWS, LANES) for x in fields[:6]] + fields[6:]
    kinds = [F32] * 5 + [jnp.int32] + [F32] * 2
    state_scratch = lambda rows: [pltpu.VMEM((rows,) + tile, F32) for _ in range(6)]

    rows_a, rows_b = call(
        rows_kernel,
        fields,
        [(21,) + tile, (27,) + tile],
        [pltpu.VMEM((2, LEVELS) + tile, kind) for kind in kinds[:6]]
        + [pltpu.VMEM((2,) + tile, F32)] * 2
        + [pltpu.SemaphoreType.DMA((8, 2))],
        far=True,
        limit=54,
    )
    pairs_a, pairs_b = lat_pairs(lat, lon)
    got_b = lax.ppermute(rows_b, axes, pairs_b)
    got_a = lax.ppermute(rows_a, axes, pairs_a)
    inner, own, msgs, rims = call(
        interior_kernel,
        flat,
        [(4, ROWS + 2) + tile, (2, 7, BLOCK) + tile, (2, 2 * BLOCK) + tile, (7, 16) + tile],
        geo_scratch(ROWS + 2),
        flops=40_000_000,
        limit=50,
    )
    cols_a, cols_b = call(columns_kernel, [msgs, got_a, got_b], [(2 * BLOCK,) + tile] * 2)
    pairs_a, pairs_b = lon_pairs(lat, lon)
    lon_b = lax.ppermute(cols_b, axes, pairs_b)
    lon_a = lax.ppermute(cols_a, axes, pairs_a)
    (strips,) = call(
        rows_strip_kernel,
        [rims, got_a, got_b, hinge],
        [(4, 2 * HALO) + tile],
        state_scratch(NS_ROWS) + geo_scratch(NS_ROWS),
        smem_last=True,
        flops=10_000_000,
    )
    outs = call(
        columns_strip_kernel,
        [own, lon_a, lon_b, got_a, got_b, inner, strips, hinge],
        [(LEVELS, ROWS, LANES)] * 5,
        state_scratch(WE_ROWS)
        + geo_scratch(WE_ROWS)
        + [pltpu.VMEM((LEVELS, ROWS, LANES), F32)] * 5
        + [pltpu.SemaphoreType.DMA((5, 8))],
        out_far=True,
        smem_last=True,
        flops=10_000_000,
    )
    return tuple(outs)


def solution(mesh):
    field = P(None, "lat", "lon")
    flat = P("lat", "lon")
    return jax.shard_map(
        on_device,
        mesh=mesh,
        in_specs=(field, field, field, field, flat, flat, field, field, P()),
        out_specs=(field,) * 5,
        check_vma=False,
    )
```

```python
import jax
import jax.numpy as jnp
from jax import lax
from jax.experimental import pallas as pl
from jax.experimental.pallas import tpu as pltpu
from jax.sharding import PartitionSpec as P

F32 = jnp.float32
NSTEP = 4
LEVELS = 8
ROWS = 64
LANES = 128
HALO = 4
BLOCK = 9
GROUP = 16

time_step = 0.2
diffusivity = 0.4
eos_alpha = 0.1655
eos_beta = 0.76554
eos_lambda_one = 0.05952
eos_lambda_two = 0.00054914
eos_mu_one = 0.0001497
eos_mu_two = 1.109e-05
eos_cross = 0.0024341

SIGNS = (1.0, 1.0, -1.0, -1.0)


def roll(x, shift):
    shift = shift % LANES
    return pltpu.roll(x, shift, 1) if shift else x


def lanes():
    return lax.broadcasted_iota(jnp.int32, (LEVELS, LANES), 1)


def levels():
    return lax.broadcasted_iota(jnp.int32, (LEVELS, LANES), 0)


def mirrored(x, width):
    return jnp.take_along_axis(x, lanes() ^ (width - 1), axis=1, mode="promise_in_bounds")


def eos_terms():
    depth = 100.0 * (levels().astype(F32) + 0.5)
    return -eos_alpha * (1.0 + eos_mu_one * depth), eos_beta * (1.0 - eos_mu_two * depth)


def density_of(heat, salt, terms):
    heat_term, salt_term = terms
    return heat * (heat_term - (0.5 * eos_alpha * eos_lambda_one) * heat - eos_cross * salt) + salt * (
        salt_term - (0.5 * eos_beta * eos_lambda_two) * salt
    )


def pressure_of(heat, salt, half_depth, terms):
    half = density_of(heat, salt, terms) * half_depth
    level = levels()
    total = half
    for shift in (1, 2, 4):
        total = total + jnp.where(level >= shift, pltpu.roll(total, shift, 0), 0.0)
    return total + total - half


def geometry_row(geo, row, east0, north0, east1, north1):
    half0 = geo["half"][row]
    half1 = geo["half"][row + 1]
    half_e = roll(half0, -1)
    span = 2.0 / (east0 + roll(east0, -1))
    side = 0.5 * (north0 + roll(north0, -1))
    open_e = jnp.minimum(half0, half_e) > 0.0
    area = jnp.where(open_e, side * (half0 + half_e), 0.0)
    geo["area_e"][row] = area
    geo["cond_e"][row] = diffusivity * area * span
    geo["open_e"][row] = jnp.where(open_e, 1.0, 0.0)
    geo["push_e"][row] = time_step * span
    span = 2.0 / (north0 + north1)
    side = 0.5 * (east0 + east1)
    open_n = jnp.minimum(half0, half1) > 0.0
    area = jnp.where(open_n, side * (half0 + half1), 0.0)
    geo["area_n"][row] = area
    geo["cond_n"][row] = diffusivity * area * span
    geo["open_n"][row] = jnp.where(open_n, 1.0, 0.0)
    geo["push_n"][row] = time_step * span
    geo["inv"][row] = (0.5 * time_step) / (east0 * north0 * jnp.where(half0 > 0.0, half0, 1.0))


def march(state, geo, chains):
    terms = eos_terms()

    def north_face(row, speed):
        flow = geo["area_n"][row] * speed
        ahead = jnp.maximum(flow, 0.0) + geo["cond_n"][row]
        return ahead, flow - ahead

    def begin(row):
        before = tuple(ref[row - 1] for ref in state)
        here = tuple(ref[row] for ref in state)
        return before + here + north_face(row - 1, before[3]) + (pressure_of(here[0], here[1], geo["half"][row], terms),)

    def advance(row, carry):
        before, here = carry[0:4], carry[4:8]
        south_p, south_m, press = carry[8:]
        north = tuple(ref[row + 1] for ref in state)
        press_n = pressure_of(north[0], north[1], geo["half"][row + 1], terms)
        north_p, north_m = north_face(row, here[3])
        flow = geo["area_e"][row] * here[2]
        east_p = jnp.maximum(flow, 0.0) + geo["cond_e"][row]
        east_m = flow - east_p
        west_p, west_m = roll(east_p, 1), roll(east_m, 1)
        inv = geo["inv"][row]
        keep = 1.0 - inv * ((east_p - west_m) + (north_p - south_m))
        c_e, c_w, c_n, c_s = inv * east_m, inv * west_p, inv * north_m, inv * south_p
        new = [
            keep * c + (c_w * roll(c, 1) + c_s * s) - (c_e * roll(c, -1) + c_n * n)
            for c, s, n in zip(here, before, north)
        ]
        new[2] = (new[2] + (press - roll(press, -1)) * geo["push_e"][row]) * geo["open_e"][row]
        new[3] = (new[3] + (press - press_n) * geo["push_n"][row]) * geo["open_n"][row]
        for ref, value in zip(state, new):
            ref[row] = value
        return here + north + (north_p, north_m, press_n)

    carries = [begin(first) for first, _ in chains]
    for u in range(max(count for _, count in chains)):
        for index, (first, count) in enumerate(chains):
            if u < count:
                carries[index] = advance(first + u, carries[index])


GEO = ("half", "area_e", "cond_e", "open_e", "push_e", "area_n", "cond_n", "open_n", "push_n", "inv")


def geo_scratch(rows):
    return [pltpu.VMEM((rows, LEVELS, LANES), F32) for _ in GEO]


def column_of(ref, row):
    return ref[pl.ds(row, LEVELS, stride=ref.shape[0] // LEVELS), :]


def wide(ref, row):
    return jnp.broadcast_to(ref[pl.ds(row, 1), :], (LEVELS, LANES))


def own_row(refs, row):
    heat, salt, east, north, thick, water = [column_of(ref, row) for ref in refs[:6]]
    wet = water.astype(F32)
    return heat * wet, salt * wet, east, north, 0.5 * (thick * wet)


def rows_kernel(*refs):
    ins, (out_a, out_b) = refs[:8], refs[8:10]
    rims, sems = refs[10:18], refs[18]
    copies = []
    for f, (src, dst) in enumerate(zip(ins, rims)):
        for side, row in ((0, 0), (1, ROWS - 8)):
            if f < 6:
                pair = src.at[:, pl.ds(row, 8), :], dst.at[side]
            else:
                pair = src.at[pl.ds(row, 8), :], dst.at[side]
            copies.append(pltpu.make_async_copy(*pair, sems.at[f, side]))
    for copy in copies:
        copy.start()
    out_b[25] = jnp.ones((LEVELS, LANES), F32)
    out_b[26] = jnp.ones((LEVELS, LANES), F32)
    for copy in copies:
        copy.wait()
    even = lax.rem(lax.axis_index("lat"), 2) == 0
    side_a = jnp.where(even, 1, 0)
    row_a = jnp.where(even, HALO, 0)
    side_b = jnp.where(even, 0, 1)
    row_b = jnp.where(even, 0, HALO - 1)
    for out, side, row, count, flat in ((out_a, side_a, row_a, HALO, 0), (out_b, side_b, row_b, HALO + 1, 1)):
        cut = [ref.at[side].reshape(LEVELS * 8, LANES) for ref in rims[:6]]
        for i in range(count):
            for f, value in enumerate(own_row(cut, row + i)):
                out[5 * i + f] = value
            for f in range(2):
                place = (20, HALO * f + i) if flat == 0 else (25 + f, i)
                out[place[0], pl.ds(place[1], 1), :] = rims[6 + f][side, pl.ds(row + i, 1), :]


def halo_rows(got_a, got_b):
    even = lax.rem(lax.axis_index("lat"), 2) == 0

    def spread(row):
        return jnp.broadcast_to(row, (LEVELS, LANES))

    def read_a(i, f):
        if f < 5:
            return got_a[5 * i + f]
        return spread(got_a[20, pl.ds(HALO * (f - 5) + i, 1), :])

    def read_b(i, f):
        if f < 5:
            return got_b[5 * i + f]
        return spread(got_b[20 + f, pl.ds(i, 1), :])

    def sane(value, f):
        return value if f < 5 else jnp.where(value > 0.0, value, 1.0)

    def south(i, f):
        return sane(jnp.where(even, read_b(i + 1, f), read_a(i, f)), f)

    def north(i, f):
        return sane(jnp.where(even, read_a(i, f), read_b(i, f)), f)

    def fold(i, f):
        return sane(read_b(i, f), f)

    return south, north, fold


def interior_kernel(*refs):
    ins = refs[:8]
    state_out, own, msgs, rims = refs[8:12]
    state = [state_out.at[f] for f in range(4)]
    geo = dict(zip(GEO, refs[12:22]))
    blank = jnp.zeros((LEVELS, LANES), F32)
    for ref in state + [geo["half"]]:
        ref[0] = blank
        ref[ROWS + 1] = blank

    def take(row, carry):
        values = own_row(ins, row)
        for ref, value in zip(state, values):
            ref[row + 1] = value
        geo["half"][row + 1] = values[4]
        return carry

    lax.fori_loop(0, ROWS, take, 0, unroll=8)
    for i in range(8):
        for place, row in ((i, i), (8 + i, ROWS - 8 + i)):
            for f in range(4):
                rims[f, place] = state[f][row + 1]
            rims[4, place] = geo["half"][row + 1]
            rims[5, place] = wide(ins[6], row)
            rims[6, place] = wide(ins[7], row)

    lane = lanes()
    part = (lane // HALO) % (GROUP // HALO)

    def pack(g, carry):
        packs = []
        for f in range(7):
            west = east = jnp.zeros((LEVELS, LANES), F32)
            for q in range(8):
                row = jnp.clip(BLOCK * q + g - HALO, 0, ROWS - 1)
                if f < 4:
                    value = state[f][row + 1]
                elif f == 4:
                    value = geo["half"][row + 1]
                else:
                    value = wide(ins[f + 1], row)
                here = (lane // GROUP) == q
                west = jnp.where(here, roll(value, GROUP * q + HALO), west)
                east = jnp.where(here, roll(value, GROUP * q + 12), east)
            own[0, f, g] = west
            own[1, f, g] = east
            packs.append((west, east))
        for side in range(2):
            for half, first in ((0, 0), (1, 4)):
                message = jnp.zeros((LEVELS, LANES), F32)
                for f in range(4 if half == 0 else 3):
                    value = packs[first + f][side]
                    shift = HALO * f - (HALO if side == 0 else 2 * HALO)
                    message = jnp.where(part == f, roll(value, shift), message)
                msgs[side, BLOCK * half + g] = message
        return carry

    lax.fori_loop(0, BLOCK, pack, 0, unroll=3)

    def shape(row, carry):
        geometry_row(geo, row + 1, wide(ins[6], row), wide(ins[7], row), wide(ins[6], row + 1), wide(ins[7], row + 1))
        return carry

    lax.fori_loop(0, ROWS - 1, shape, 0, unroll=7)

    def step(s, carry):
        march(state, geo, ((2, ROWS - 2),))
        return carry

    lax.fori_loop(1, NSTEP + 1, step, 0)


def columns_kernel(msgs, got_a, got_b, out_a, out_b):
    even = lax.rem(lax.axis_index("lon"), 2) == 0
    top = lax.axis_index("lat") == lax.axis_size("lat") - 1
    south, north, fold = halo_rows(got_a, got_b)
    lane = lanes()
    part = (lane // HALO) % (GROUP // HALO)
    for half, first in ((0, 0), (1, 4)):
        for g in range(BLOCK):
            slot = BLOCK * half + g
            west, east = msgs[0, slot], msgs[1, slot]
            if g != HALO:
                add_w = add_e = jnp.zeros((LEVELS, LANES), F32)
                base = 0 if g < HALO else 7 * GROUP
                for f in range(4 if half == 0 else 3):
                    if g < HALO:
                        value = south(g, first + f)
                    else:
                        value = jnp.where(top, fold(g - 4, first + f), north(g - 5, first + f))
                    add_w = jnp.where(part == f, roll(value, base + HALO * f), add_w)
                    add_e = jnp.where(part == f, roll(value, base + HALO * f + HALO), add_e)
                if g < HALO:
                    here = lane < GROUP
                else:
                    here = lane >= 7 * GROUP
                    add_w, add_e = jnp.where(top, add_e, add_w), jnp.where(top, add_w, add_e)
                west = jnp.where(here, add_w, west)
                east = jnp.where(here, add_e, east)
            out_a[slot] = jnp.where(even, east, west)
            out_b[slot] = jnp.where(even, west, east)


SOUTH, NORTH, FOLD, NS_ROWS = 0, 12, 24, 30


def rows_strip_kernel(*refs):
    rims, got_a, got_b, hinge, out = refs[:5]
    state = refs[5:9]
    east_w, north_w = refs[9:11]
    geo = dict(zip(GEO, refs[11:]))
    top = lax.axis_index("lat") == lax.axis_size("lat") - 1
    pivot = hinge[0]
    south, north, fold = halo_rows(got_a, got_b)
    fields = list(state) + [geo["half"], east_w, north_w]
    for f, ref in enumerate(fields):
        for i in range(HALO):
            ref[SOUTH + i] = south(i, f)
            ref[NORTH + 8 + i] = north(i, f)
            ref[FOLD + i] = fold(i, f)
        ref[FOLD + HALO] = fold(HALO, f)
        for i in range(8):
            ref[SOUTH + HALO + i] = rims[f, i]
            ref[NORTH + i] = rims[f, 8 + i]

    def refold(ref, sign):
        ghost = sign * mirrored(ref[FOLD + 4 - pivot], LANES)
        ref[FOLD + 5] = sign * mirrored(ref[NORTH + 7 - pivot], LANES)
        ref[NORTH + 8] = jnp.where(top, ghost, ref[NORTH + 8])

    for ref in fields[4:]:
        refold(ref, 1.0)
    for row in (*range(SOUTH, SOUTH + 11), *range(NORTH, NORTH + 11), *range(FOLD, FOLD + 5)):
        geometry_row(geo, row, east_w[row], north_w[row], east_w[row + 1], north_w[row + 1])

    for s in range(1, NSTEP + 1):
        for ref, sign in zip(state, SIGNS):
            refold(ref, sign)
        chains = [(SOUTH + s, 12 - 2 * s), (NORTH + s, 12 - 2 * s)]
        if s < NSTEP:
            chains.append((FOLD + s, 5 - s))
        march(state, geo, chains)

    for f, ref in enumerate(state):
        for i in range(HALO):
            out[f, i] = ref[SOUTH + HALO + i]
            out[f, HALO + i] = ref[NORTH + HALO + i]


WEST, EAST, FOLDS, WE_ROWS = 0, 11, 22, 28


def columns_strip_kernel(*refs):
    own, lon_b, lon_a, got_a, got_b, inner, strips, hinge = refs[:8]
    outs = refs[8:13]
    state = refs[13:17]
    east_w, north_w = refs[17:19]
    geo = dict(zip(GEO, refs[19:29]))
    stage, sems = refs[29:34], refs[34]
    even = lax.rem(lax.axis_index("lon"), 2) == 0
    top = lax.axis_index("lat") == lax.axis_size("lat") - 1
    below = hinge[0] == 1
    south, north, fold = halo_rows(got_a, got_b)
    fields = list(state) + [geo["half"], east_w, north_w]
    lane = lanes()
    inside = lane % GROUP

    def message(side, f, g):
        slot = g if f < 4 else BLOCK + g
        a, b = lon_a[slot], lon_b[slot]
        return jnp.where(even, b, a) if side == 0 else jnp.where(even, a, b)

    for g in range(BLOCK):
        for f, ref in enumerate(fields):
            west, east = own[0, f, g], own[1, f, g]
            if g < HALO:
                value = south(g, f)
                west = jnp.where(lane < GROUP, roll(value, HALO), west)
                east = jnp.where(lane < GROUP, roll(value, 12), east)
            elif g > HALO:
                value = north(g - 5, f)
                west = jnp.where(lane >= 7 * GROUP, roll(value, 7 * GROUP + HALO), west)
                east = jnp.where(lane >= 7 * GROUP, roll(value, 7 * GROUP + 12), east)
            shift = -HALO * (f % 4)
            west = jnp.where(inside < HALO, roll(message(0, f, g), shift), west)
            east = jnp.where(inside >= 12, roll(message(1, f, g), shift + 12), east)
            if f > 4:
                west = jnp.where(west > 0.0, west, 1.0)
                east = jnp.where(east > 0.0, east, 1.0)
            ref[WEST + 1 + g] = west
            ref[EAST + 1 + g] = east

    def rewrap(ref):
        for base in (WEST, EAST):
            ref[base] = roll(ref[base + 9], GROUP)
            ref[base + 10] = roll(ref[base + 1], -GROUP)

    def refold(ref, sign):
        ghost = sign * mirrored(jnp.where(below, ref[FOLDS + 3], ref[FOLDS + 4]), GROUP)
        from_e = jnp.where(below, ref[EAST + 4], ref[EAST + 5])
        from_w = jnp.where(below, ref[WEST + 4], ref[WEST + 5])
        back = jnp.where(lane < GROUP, roll(from_e, GROUP), roll(from_w, 2 * GROUP))
        ref[FOLDS + 5] = sign * mirrored(back, GROUP)
        here = (lane >= 7 * GROUP) & top
        ref[WEST + 6] = jnp.where(here, roll(ghost, 6 * GROUP), ref[WEST + 6])
        ref[EAST + 6] = jnp.where(here, roll(ghost, 7 * GROUP), ref[EAST + 6])

    for i in range(HALO + 1):
        for f, ref in enumerate(fields):
            value = fold(i, f)
            value = jnp.where(lane < GROUP, roll(value, HALO), roll(value, 28))
            if i > 0:
                slot = HALO + i
                corner = 7 * GROUP + HALO * (f % 4)
                value = jnp.where(lane < HALO, roll(message(1, f, slot), -corner), value)
                other = roll(message(0, f, slot), 28 - corner)
                value = jnp.where((lane >= 28) & (lane < 32), other, value)
            if f > 4:
                value = jnp.where(value > 0.0, value, 1.0)
            ref[FOLDS + i] = value
    for ref in fields[4:]:
        refold(ref, 1.0)
        rewrap(ref)
    for row in (*range(WEST, WEST + 10), *range(EAST, EAST + 10), *range(FOLDS, FOLDS + 5)):
        geometry_row(geo, row, east_w[row], north_w[row], east_w[row + 1], north_w[row + 1])

    def step(s, carry):
        for ref, sign in zip(state, SIGNS):
            refold(ref, sign)
            rewrap(ref)
        march(state, geo, ((WEST + 1, BLOCK), (EAST + 1, BLOCK), (FOLDS + 1, 4)))
        return carry

    lax.fori_loop(1, NSTEP + 1, step, 0)

    for ref in state:
        for g in range(BLOCK):
            ref[WEST + 1 + g] = jnp.where(inside < HALO, roll(ref[EAST + 1 + g], -8), ref[WEST + 1 + g])
    rim = (lane < HALO) | (lane >= LANES - HALO)
    terms = eos_terms()

    copies = []
    for row in range(ROWS):
        q, g = divmod(row + HALO, BLOCK)
        if HALO <= row < ROWS - HALO:
            bases = [inner[f, row + 1] for f in range(4)]
        else:
            place = row if row < HALO else row - (ROWS - 2 * HALO)
            bases = [strips[f, place] for f in range(4)]
        new = [
            jnp.where(rim, roll(ref[WEST + 1 + g], -(GROUP * q + HALO)), base) for ref, base in zip(state, bases)
        ]
        new.append(density_of(new[0], new[1], terms))
        for ref, value in zip(stage, new):
            ref.reshape(LEVELS * ROWS, LANES)[pl.ds(row, LEVELS, stride=ROWS), :] = value
        if row % 16 == 15:
            rows = pl.ds(row - 15, 16)
            for f in range(5):
                copy = pltpu.make_async_copy(stage[f].at[:, rows, :], outs[f].at[:, rows, :], sems.at[f, row // 16])
                copy.start()
                copies.append(copy)
    for copy in copies:
        copy.wait()


def call(kernel, ins, outs, scratch=(), smem_last=False, far=False, out_far=False, flops=0):
    place = pltpu.HBM if far else pltpu.VMEM
    specs = [pl.BlockSpec(memory_space=place) for _ in ins]
    ins = [pltpu.with_memory_space_constraint(x, place) for x in ins[:-1]] + [ins[-1]]
    if smem_last:
        specs[-1] = pl.BlockSpec(memory_space=pltpu.SMEM)
    else:
        ins[-1] = pltpu.with_memory_space_constraint(ins[-1], place)
    if out_far:
        out_shape = [jax.ShapeDtypeStruct(shape, F32) for shape in outs]
    else:
        out_shape = [pltpu.VMEM(shape, F32) for shape in outs]
    return pl.pallas_call(
        kernel,
        out_shape=out_shape,
        in_specs=specs,
        out_specs=[pl.BlockSpec(memory_space=pltpu.HBM if out_far else pltpu.VMEM) for _ in outs],
        scratch_shapes=list(scratch),
        compiler_params=pltpu.CompilerParams(vmem_limit_bytes=40 * 1024 * 1024),
        cost_estimate=pl.CostEstimate(flops=flops, bytes_accessed=2_000_000, transcendentals=0),
    )(*ins)


def lat_pairs(lat, lon):
    first = [(a * lon + o, (a ^ 1) * lon + o) for a in range(lat) for o in range(lon)]
    second = [
        (a * lon + o, (a + 1 if a % 2 else a - 1) * lon + o) for a in range(1, lat - 1) for o in range(lon)
    ]
    second += [((lat - 1) * lon + o, (lat - 1) * lon + lon - 1 - o) for o in range(lon)]
    return first, second


def lon_pairs(lat, lon):
    first = [(a * lon + o, a * lon + (o ^ 1)) for a in range(lat) for o in range(lon)]
    second = [
        (a * lon + o, a * lon + ((o + 1) if o % 2 else (o - 1)) % lon) for a in range(lat) for o in range(lon)
    ]
    return first, second


def on_device(*args):
    lat, lon = lax.axis_size("lat"), lax.axis_size("lon")
    axes = ("lat", "lon")
    hinge = args[8]
    tile = (LEVELS, LANES)
    fields = [*args[:4], args[6], args[7], args[4], args[5]]
    flat = [x.reshape(LEVELS * ROWS, LANES) for x in fields[:6]] + fields[6:]
    kinds = [F32] * 5 + [jnp.int32] + [F32] * 2
    state_scratch = lambda rows: [pltpu.VMEM((rows,) + tile, F32) for _ in range(6)]

    rows_a, rows_b = call(
        rows_kernel,
        fields,
        [(21,) + tile, (27,) + tile],
        [pltpu.VMEM((2, LEVELS) + tile, kind) for kind in kinds[:6]]
        + [pltpu.VMEM((2,) + tile, F32)] * 2
        + [pltpu.SemaphoreType.DMA((8, 2))],
        far=True,
    )
    pairs_a, pairs_b = lat_pairs(lat, lon)
    got_b = lax.ppermute(rows_b, axes, pairs_b)
    got_a = lax.ppermute(rows_a, axes, pairs_a)
    inner, own, msgs, rims = call(
        interior_kernel,
        flat,
        [(4, ROWS + 2) + tile, (2, 7, BLOCK) + tile, (2, 2 * BLOCK) + tile, (7, 16) + tile],
        geo_scratch(ROWS + 2),
        flops=40_000_000,
    )
    cols_a, cols_b = call(columns_kernel, [msgs, got_a, got_b], [(2 * BLOCK,) + tile] * 2)
    pairs_a, pairs_b = lon_pairs(lat, lon)
    lon_b = lax.ppermute(cols_b, axes, pairs_b)
    lon_a = lax.ppermute(cols_a, axes, pairs_a)
    (strips,) = call(
        rows_strip_kernel,
        [rims, got_a, got_b, hinge],
        [(4, 2 * HALO) + tile],
        state_scratch(NS_ROWS) + geo_scratch(NS_ROWS),
        smem_last=True,
        flops=10_000_000,
    )
    outs = call(
        columns_strip_kernel,
        [own, lon_b, lon_a, got_a, got_b, inner, strips, hinge],
        [(LEVELS, ROWS, LANES)] * 5,
        state_scratch(WE_ROWS)
        + geo_scratch(WE_ROWS)
        + [pltpu.VMEM((LEVELS, ROWS, LANES), F32)] * 5
        + [pltpu.SemaphoreType.DMA((5, 4))],
        out_far=True,
        smem_last=True,
        flops=10_000_000,
    )
    return tuple(outs)


def solution(mesh):
    field = P(None, "lat", "lon")
    flat = P("lat", "lon")
    return jax.shard_map(
        on_device,
        mesh=mesh,
        in_specs=(field, field, field, field, flat, flat, field, field, P()),
        out_specs=(field,) * 5,
        check_vma=False,
    )
```

```python
import jax
import jax.numpy as jnp
from jax import lax
from jax.experimental import pallas as pl
from jax.experimental.pallas import tpu as pltpu
from jax.sharding import PartitionSpec as P

F32 = jnp.float32
NSTEP = 4
LEVELS = 8
ROWS = 64
LANES = 128
HALO = 4
BLOCK = 9
GROUP = 16

time_step = 0.2
diffusivity = 0.4
eos_alpha = 0.1655
eos_beta = 0.76554
eos_lambda_one = 0.05952
eos_lambda_two = 0.00054914
eos_mu_one = 0.0001497
eos_mu_two = 1.109e-05
eos_cross = 0.0024341

SIGNS = (1.0, 1.0, -1.0, -1.0)


def roll(x, shift):
    shift = shift % LANES
    return pltpu.roll(x, shift, 1) if shift else x


def lanes():
    return lax.broadcasted_iota(jnp.int32, (LEVELS, LANES), 1)


def levels():
    return lax.broadcasted_iota(jnp.int32, (LEVELS, LANES), 0)


def mirrored(x, width):
    return jnp.take_along_axis(x, lanes() ^ (width - 1), axis=1, mode="promise_in_bounds")


def eos_terms():
    depth = 100.0 * (levels().astype(F32) + 0.5)
    return -eos_alpha * (1.0 + eos_mu_one * depth), eos_beta * (1.0 - eos_mu_two * depth)


def density_of(heat, salt, terms):
    heat_term, salt_term = terms
    return heat * (heat_term - (0.5 * eos_alpha * eos_lambda_one) * heat - eos_cross * salt) + salt * (
        salt_term - (0.5 * eos_beta * eos_lambda_two) * salt
    )


def pressure_of(heat, salt, half_depth, terms):
    half = density_of(heat, salt, terms) * half_depth
    level = levels()
    total = half
    for shift in (1, 2, 4):
        total = total + jnp.where(level >= shift, pltpu.roll(total, shift, 0), 0.0)
    return total + total - half


def geometry_row(geo, row, east0, north0, east1, north1):
    half0 = geo["half"][row]
    half1 = geo["half"][row + 1]
    half_e = roll(half0, -1)
    span = 2.0 / (east0 + roll(east0, -1))
    side = 0.5 * (north0 + roll(north0, -1))
    open_e = jnp.minimum(half0, half_e) > 0.0
    area = jnp.where(open_e, side * (half0 + half_e), 0.0)
    geo["area_e"][row] = area
    geo["cond_e"][row] = diffusivity * area * span
    geo["open_e"][row] = jnp.where(open_e, 1.0, 0.0)
    geo["push_e"][row] = time_step * span
    span = 2.0 / (north0 + north1)
    side = 0.5 * (east0 + east1)
    open_n = jnp.minimum(half0, half1) > 0.0
    area = jnp.where(open_n, side * (half0 + half1), 0.0)
    geo["area_n"][row] = area
    geo["cond_n"][row] = diffusivity * area * span
    geo["open_n"][row] = jnp.where(open_n, 1.0, 0.0)
    geo["push_n"][row] = time_step * span
    geo["inv"][row] = (0.5 * time_step) / (east0 * north0 * jnp.where(half0 > 0.0, half0, 1.0))


def march(state, geo, chains, target=None):
    terms = eos_terms()

    def north_face(row, speed):
        flow = geo["area_n"][row] * speed
        ahead = jnp.maximum(flow, 0.0) + geo["cond_n"][row]
        return ahead, flow - ahead

    def begin(row):
        before = tuple(ref[row - 1] for ref in state)
        here = tuple(ref[row] for ref in state)
        return before + here + north_face(row - 1, before[3]) + (pressure_of(here[0], here[1], geo["half"][row], terms),)

    def advance(row, carry):
        before, here = carry[0:4], carry[4:8]
        south_p, south_m, press = carry[8:]
        north = tuple(ref[row + 1] for ref in state)
        press_n = pressure_of(north[0], north[1], geo["half"][row + 1], terms)
        north_p, north_m = north_face(row, here[3])
        flow = geo["area_e"][row] * here[2]
        east_p = jnp.maximum(flow, 0.0) + geo["cond_e"][row]
        east_m = flow - east_p
        west_p, west_m = roll(east_p, 1), roll(east_m, 1)
        inv = geo["inv"][row]
        keep = 1.0 - inv * ((east_p - west_m) + (north_p - south_m))
        c_e, c_w, c_n, c_s = inv * east_m, inv * west_p, inv * north_m, inv * south_p
        new = [
            keep * c + (c_w * roll(c, 1) + c_s * s) - (c_e * roll(c, -1) + c_n * n)
            for c, s, n in zip(here, before, north)
        ]
        new[2] = (new[2] + (press - roll(press, -1)) * geo["push_e"][row]) * geo["open_e"][row]
        new[3] = (new[3] + (press - press_n) * geo["push_n"][row]) * geo["open_n"][row]
        for ref, value in zip(state if target is None else target, new):
            ref[row] = value
        return here + north + (north_p, north_m, press_n)

    carries = [begin(first) for first, _ in chains]
    for u in range(max(count for _, count in chains)):
        for index, (first, count) in enumerate(chains):
            if u < count:
                carries[index] = advance(first + u, carries[index])


GEO = ("half", "area_e", "cond_e", "open_e", "push_e", "area_n", "cond_n", "open_n", "push_n", "inv")


def geo_scratch(rows):
    return [pltpu.VMEM((rows, LEVELS, LANES), F32) for _ in GEO]


def column_of(ref, row):
    return ref[pl.ds(row, LEVELS, stride=ref.shape[0] // LEVELS), :]


def wide(ref, row):
    return jnp.broadcast_to(ref[pl.ds(row, 1), :], (LEVELS, LANES))


def own_row(refs, row):
    heat, salt, east, north, thick, water = [column_of(ref, row) for ref in refs[:6]]
    wet = water.astype(F32)
    return heat * wet, salt * wet, east, north, 0.5 * (thick * wet)


def rows_kernel(*refs):
    ins, (out_a, out_b) = refs[:8], refs[8:10]
    rims, sems = refs[10:18], refs[18]
    copies = []
    for f, (src, dst) in enumerate(zip(ins, rims)):
        for side, row in ((0, 0), (1, ROWS - 8)):
            if f < 6:
                pair = src.at[:, pl.ds(row, 8), :], dst.at[side]
            else:
                pair = src.at[pl.ds(row, 8), :], dst.at[side]
            copies.append(pltpu.make_async_copy(*pair, sems.at[f, side]))
    for copy in copies:
        copy.start()
    out_b[25] = jnp.ones((LEVELS, LANES), F32)
    out_b[26] = jnp.ones((LEVELS, LANES), F32)
    for copy in copies:
        copy.wait()
    even = lax.rem(lax.axis_index("lat"), 2) == 0
    side_a = jnp.where(even, 1, 0)
    row_a = jnp.where(even, HALO, 0)
    side_b = jnp.where(even, 0, 1)
    row_b = jnp.where(even, 0, HALO - 1)
    for out, side, row, count, flat in ((out_a, side_a, row_a, HALO, 0), (out_b, side_b, row_b, HALO + 1, 1)):
        cut = [ref.at[side].reshape(LEVELS * 8, LANES) for ref in rims[:6]]
        for i in range(count):
            for f, value in enumerate(own_row(cut, row + i)):
                out[5 * i + f] = value
            for f in range(2):
                place = (20, HALO * f + i) if flat == 0 else (25 + f, i)
                out[place[0], pl.ds(place[1], 1), :] = rims[6 + f][side, pl.ds(row + i, 1), :]


def halo_rows(got_a, got_b):
    even = lax.rem(lax.axis_index("lat"), 2) == 0

    def spread(row):
        return jnp.broadcast_to(row, (LEVELS, LANES))

    def read_a(i, f):
        if f < 5:
            return got_a[5 * i + f]
        return spread(got_a[20, pl.ds(HALO * (f - 5) + i, 1), :])

    def read_b(i, f):
        if f < 5:
            return got_b[5 * i + f]
        return spread(got_b[20 + f, pl.ds(i, 1), :])

    def sane(value, f):
        return value if f < 5 else jnp.where(value > 0.0, value, 1.0)

    def south(i, f):
        return sane(jnp.where(even, read_b(i + 1, f), read_a(i, f)), f)

    def north(i, f):
        return sane(jnp.where(even, read_a(i, f), read_b(i, f)), f)

    def fold(i, f):
        return sane(read_b(i, f), f)

    return south, north, fold


def interior_kernel(*refs):
    ins = refs[:8]
    state_out, own, msgs, rims, geo_out = refs[8:13]
    state = [state_out.at[f] for f in range(4)]
    geo = {name: geo_out.at[index] for index, name in enumerate(GEO)}
    spread = refs[13:15]
    blank = jnp.zeros((LEVELS, LANES), F32)
    for ref in state + [geo["half"]]:
        ref[0] = blank
        ref[ROWS + 1] = blank

    def take(row, carry):
        values = own_row(ins, row)
        for ref, value in zip(state, values):
            ref[row + 1] = value
        geo["half"][row + 1] = values[4]
        spread[0][row + 1] = wide(ins[6], row)
        spread[1][row + 1] = wide(ins[7], row)
        return carry

    lax.fori_loop(0, ROWS, take, 0, unroll=8)
    for i in range(8):
        for place, row in ((i, i), (8 + i, ROWS - 8 + i)):
            for f in range(4):
                rims[f, place] = state[f][row + 1]
            rims[4, place] = geo["half"][row + 1]
            rims[5, place] = spread[0][row + 1]
            rims[6, place] = spread[1][row + 1]

    lane = lanes()
    part = (lane >> 2) & 3

    def pack(g, carry):
        packs = []
        for f in range(7):
            west = east = jnp.zeros((LEVELS, LANES), F32)
            for q in range(8):
                row = jnp.clip(BLOCK * q + g - HALO, 0, ROWS - 1)
                if f < 4:
                    value = state[f][row + 1]
                elif f == 4:
                    value = geo["half"][row + 1]
                else:
                    value = spread[f - 5][row + 1]
                here = (lane >> 4) == q
                west = jnp.where(here, roll(value, GROUP * q + HALO), west)
                east = jnp.where(here, roll(value, GROUP * q + 12), east)
            own[0, f, g] = west
            own[1, f, g] = east
            packs.append((west, east))
        for side in range(2):
            for half, first in ((0, 0), (1, 4)):
                message = jnp.zeros((LEVELS, LANES), F32)
                for f in range(4 if half == 0 else 3):
                    value = packs[first + f][side]
                    shift = HALO * f - (HALO if side == 0 else 2 * HALO)
                    message = jnp.where(part == f, roll(value, shift), message)
                msgs[side, BLOCK * half + g] = message
        return carry

    lax.fori_loop(0, BLOCK, pack, 0, unroll=3)

    def shape(row, carry):
        geometry_row(geo, row + 1, spread[0][row + 1], spread[1][row + 1], spread[0][row + 2], spread[1][row + 2])
        return carry

    lax.fori_loop(0, ROWS - 1, shape, 0, unroll=7)

    def step(s, carry):
        march(state, geo, ((2, ROWS - 2),))
        return carry

    lax.fori_loop(1, NSTEP, step, 0)


def columns_kernel(msgs, got_a, got_b, out_a, out_b):
    even = lax.rem(lax.axis_index("lon"), 2) == 0
    top = lax.axis_index("lat") == lax.axis_size("lat") - 1
    south, north, fold = halo_rows(got_a, got_b)
    lane = lanes()
    part = (lane >> 2) & 3
    for half, first in ((0, 0), (1, 4)):
        for g in range(BLOCK):
            slot = BLOCK * half + g
            west, east = msgs[0, slot], msgs[1, slot]
            if g != HALO:
                add_w = add_e = jnp.zeros((LEVELS, LANES), F32)
                base = 0 if g < HALO else 7 * GROUP
                for f in range(4 if half == 0 else 3):
                    if g < HALO:
                        value = south(g, first + f)
                    else:
                        value = jnp.where(top, fold(g - 4, first + f), north(g - 5, first + f))
                    add_w = jnp.where(part == f, roll(value, base + HALO * f), add_w)
                    add_e = jnp.where(part == f, roll(value, base + HALO * f + HALO), add_e)
                if g < HALO:
                    here = lane < GROUP
                else:
                    here = lane >= 7 * GROUP
                    add_w, add_e = jnp.where(top, add_e, add_w), jnp.where(top, add_w, add_e)
                west = jnp.where(here, add_w, west)
                east = jnp.where(here, add_e, east)
            out_a[slot] = jnp.where(even, east, west)
            out_b[slot] = jnp.where(even, west, east)


SOUTH, NORTH, FOLD, NS_ROWS = 0, 12, 24, 30


def rows_strip_kernel(*refs):
    inner, inner_geo, rims, got_a, got_b, hinge, out, inner_out = refs[:8]
    state = refs[8:12]
    east_w, north_w = refs[12:14]
    geo = dict(zip(GEO, refs[14:]))
    top = lax.axis_index("lat") == lax.axis_size("lat") - 1
    pivot = hinge[0]
    south, north, fold = halo_rows(got_a, got_b)
    fields = list(state) + [geo["half"], east_w, north_w]
    for f, ref in enumerate(fields):
        for i in range(HALO):
            ref[SOUTH + i] = south(i, f)
            ref[NORTH + 8 + i] = north(i, f)
            ref[FOLD + i] = fold(i, f)
        ref[FOLD + HALO] = fold(HALO, f)
        for i in range(8):
            ref[SOUTH + HALO + i] = rims[f, i]
            ref[NORTH + i] = rims[f, 8 + i]

    def refold(ref, sign):
        ghost = sign * mirrored(ref[FOLD + 4 - pivot], LANES)
        ref[FOLD + 5] = sign * mirrored(ref[NORTH + 7 - pivot], LANES)
        ref[NORTH + 8] = jnp.where(top, ghost, ref[NORTH + 8])

    for ref in fields[4:]:
        refold(ref, 1.0)
    for row in (*range(SOUTH, SOUTH + 11), *range(NORTH, NORTH + 11), *range(FOLD, FOLD + 5)):
        geometry_row(geo, row, east_w[row], north_w[row], east_w[row + 1], north_w[row + 1])

    for s in range(1, NSTEP + 1):
        for ref, sign in zip(state, SIGNS):
            refold(ref, sign)
        chains = [(SOUTH + s, 12 - 2 * s), (NORTH + s, 12 - 2 * s)]
        if s < NSTEP:
            chains.append((FOLD + s, 5 - s))
        march(state, geo, chains)

    march(
        [inner.at[f] for f in range(4)],
        {name: inner_geo.at[index] for index, name in enumerate(GEO)},
        ((HALO + 1, ROWS - 2 * HALO),),
        [inner_out.at[f] for f in range(4)],
    )

    for f, ref in enumerate(state):
        for i in range(HALO):
            out[f, i] = ref[SOUTH + HALO + i]
            out[f, HALO + i] = ref[NORTH + HALO + i]


WEST, EAST, FOLDS, WE_ROWS = 0, 11, 22, 28


def columns_strip_kernel(*refs):
    own, lon_b, lon_a, got_a, got_b, inner, strips, hinge = refs[:8]
    outs = refs[8:13]
    state = refs[13:17]
    east_w, north_w = refs[17:19]
    geo = dict(zip(GEO, refs[19:29]))
    stage, sems = refs[29:34], refs[34]
    even = lax.rem(lax.axis_index("lon"), 2) == 0
    top = lax.axis_index("lat") == lax.axis_size("lat") - 1
    below = hinge[0] == 1
    south, north, fold = halo_rows(got_a, got_b)
    fields = list(state) + [geo["half"], east_w, north_w]
    lane = lanes()
    inside = lane & (GROUP - 1)

    def message(side, f, g):
        slot = g if f < 4 else BLOCK + g
        a, b = lon_a[slot], lon_b[slot]
        return jnp.where(even, b, a) if side == 0 else jnp.where(even, a, b)

    for g in range(BLOCK):
        for f, ref in enumerate(fields):
            west, east = own[0, f, g], own[1, f, g]
            if g < HALO:
                value = south(g, f)
                west = jnp.where(lane < GROUP, roll(value, HALO), west)
                east = jnp.where(lane < GROUP, roll(value, 12), east)
            elif g > HALO:
                value = north(g - 5, f)
                west = jnp.where(lane >= 7 * GROUP, roll(value, 7 * GROUP + HALO), west)
                east = jnp.where(lane >= 7 * GROUP, roll(value, 7 * GROUP + 12), east)
            shift = -HALO * (f % 4)
            west = jnp.where(inside < HALO, roll(message(0, f, g), shift), west)
            east = jnp.where(inside >= 12, roll(message(1, f, g), shift + 12), east)
            if f > 4:
                west = jnp.where(west > 0.0, west, 1.0)
                east = jnp.where(east > 0.0, east, 1.0)
            ref[WEST + 1 + g] = west
            ref[EAST + 1 + g] = east

    def rewrap(ref):
        for base in (WEST, EAST):
            ref[base] = roll(ref[base + 9], GROUP)
            ref[base + 10] = roll(ref[base + 1], -GROUP)

    def refold(ref, sign):
        ghost = sign * mirrored(jnp.where(below, ref[FOLDS + 3], ref[FOLDS + 4]), GROUP)
        from_e = jnp.where(below, ref[EAST + 4], ref[EAST + 5])
        from_w = jnp.where(below, ref[WEST + 4], ref[WEST + 5])
        back = jnp.where(lane < GROUP, roll(from_e, GROUP), roll(from_w, 2 * GROUP))
        ref[FOLDS + 5] = sign * mirrored(back, GROUP)
        here = (lane >= 7 * GROUP) & top
        ref[WEST + 6] = jnp.where(here, roll(ghost, 6 * GROUP), ref[WEST + 6])
        ref[EAST + 6] = jnp.where(here, roll(ghost, 7 * GROUP), ref[EAST + 6])

    for i in range(HALO + 1):
        for f, ref in enumerate(fields):
            value = fold(i, f)
            value = jnp.where(lane < GROUP, roll(value, HALO), roll(value, 28))
            if i > 0:
                slot = HALO + i
                corner = 7 * GROUP + HALO * (f % 4)
                value = jnp.where(lane < HALO, roll(message(1, f, slot), -corner), value)
                other = roll(message(0, f, slot), 28 - corner)
                value = jnp.where((lane >= 28) & (lane < 32), other, value)
            if f > 4:
                value = jnp.where(value > 0.0, value, 1.0)
            ref[FOLDS + i] = value
    for ref in fields[4:]:
        refold(ref, 1.0)
        rewrap(ref)
    for row in (*range(WEST, WEST + 10), *range(EAST, EAST + 10), *range(FOLDS, FOLDS + 5)):
        geometry_row(geo, row, east_w[row], north_w[row], east_w[row + 1], north_w[row + 1])

    def step(s, carry):
        for ref, sign in zip(state, SIGNS):
            refold(ref, sign)
            rewrap(ref)
        march(state, geo, ((WEST + 1, BLOCK), (EAST + 1, BLOCK), (FOLDS + 1, 4)))
        return carry

    lax.fori_loop(1, NSTEP + 1, step, 0)

    for ref in state:
        for g in range(BLOCK):
            ref[WEST + 1 + g] = jnp.where(inside < HALO, roll(ref[EAST + 1 + g], -8), ref[WEST + 1 + g])
    rim = (lane < HALO) | (lane >= LANES - HALO)
    terms = eos_terms()

    copies = []
    for row in range(ROWS):
        q, g = divmod(row + HALO, BLOCK)
        if HALO <= row < ROWS - HALO:
            bases = [inner[f, row + 1] for f in range(4)]
        else:
            place = row if row < HALO else row - (ROWS - 2 * HALO)
            bases = [strips[f, place] for f in range(4)]
        new = [
            jnp.where(rim, roll(ref[WEST + 1 + g], -(GROUP * q + HALO)), base) for ref, base in zip(state, bases)
        ]
        new.append(density_of(new[0], new[1], terms))
        for ref, value in zip(stage, new):
            ref.reshape(LEVELS * ROWS, LANES)[pl.ds(row, LEVELS, stride=ROWS), :] = value
        if row % 16 == 15:
            rows = pl.ds(row - 15, 16)
            for f in range(5):
                copy = pltpu.make_async_copy(stage[f].at[:, rows, :], outs[f].at[:, rows, :], sems.at[f, row // 16])
                copy.start()
                copies.append(copy)
    for copy in copies:
        copy.wait()


def call(kernel, ins, outs, scratch=(), smem_last=False, far=False, out_far=False, flops=0):
    place = pltpu.HBM if far else pltpu.VMEM
    specs = [pl.BlockSpec(memory_space=place) for _ in ins]
    ins = [pltpu.with_memory_space_constraint(x, place) for x in ins[:-1]] + [ins[-1]]
    if smem_last:
        specs[-1] = pl.BlockSpec(memory_space=pltpu.SMEM)
    else:
        ins[-1] = pltpu.with_memory_space_constraint(ins[-1], place)
    if out_far:
        out_shape = [jax.ShapeDtypeStruct(shape, F32) for shape in outs]
    else:
        out_shape = [pltpu.VMEM(shape, F32) for shape in outs]
    return pl.pallas_call(
        kernel,
        out_shape=out_shape,
        in_specs=specs,
        out_specs=[pl.BlockSpec(memory_space=pltpu.HBM if out_far else pltpu.VMEM) for _ in outs],
        scratch_shapes=list(scratch),
        compiler_params=pltpu.CompilerParams(vmem_limit_bytes=40 * 1024 * 1024),
        cost_estimate=pl.CostEstimate(flops=flops, bytes_accessed=2_000_000, transcendentals=0),
    )(*ins)


def lat_pairs(lat, lon):
    first = [(a * lon + o, (a ^ 1) * lon + o) for a in range(lat) for o in range(lon)]
    second = [
        (a * lon + o, (a + 1 if a % 2 else a - 1) * lon + o) for a in range(1, lat - 1) for o in range(lon)
    ]
    second += [((lat - 1) * lon + o, (lat - 1) * lon + lon - 1 - o) for o in range(lon)]
    return first, second


def lon_pairs(lat, lon):
    first = [(a * lon + o, a * lon + (o ^ 1)) for a in range(lat) for o in range(lon)]
    second = [
        (a * lon + o, a * lon + ((o + 1) if o % 2 else (o - 1)) % lon) for a in range(lat) for o in range(lon)
    ]
    return first, second


def on_device(*args):
    lat, lon = lax.axis_size("lat"), lax.axis_size("lon")
    axes = ("lat", "lon")
    hinge = args[8]
    tile = (LEVELS, LANES)
    fields = [*args[:4], args[6], args[7], args[4], args[5]]
    flat = [x.reshape(LEVELS * ROWS, LANES) for x in fields[:6]] + fields[6:]
    kinds = [F32] * 5 + [jnp.int32] + [F32] * 2
    state_scratch = lambda rows: [pltpu.VMEM((rows,) + tile, F32) for _ in range(6)]

    rows_a, rows_b = call(
        rows_kernel,
        fields,
        [(21,) + tile, (27,) + tile],
        [pltpu.VMEM((2, LEVELS) + tile, kind) for kind in kinds[:6]]
        + [pltpu.VMEM((2,) + tile, F32)] * 2
        + [pltpu.SemaphoreType.DMA((8, 2))],
        far=True,
    )
    pairs_a, pairs_b = lat_pairs(lat, lon)
    got_b = lax.ppermute(rows_b, axes, pairs_b)
    got_a = lax.ppermute(rows_a, axes, pairs_a)
    inner, own, msgs, rims, inner_geo = call(
        interior_kernel,
        flat,
        [(4, ROWS + 2) + tile, (2, 7, BLOCK) + tile, (2, 2 * BLOCK) + tile, (7, 16) + tile, (len(GEO), ROWS + 2) + tile],
        [pltpu.VMEM((ROWS + 2,) + tile, F32)] * 2,
        flops=40_000_000,
    )
    cols_a, cols_b = call(columns_kernel, [msgs, got_a, got_b], [(2 * BLOCK,) + tile] * 2)
    pairs_a, pairs_b = lon_pairs(lat, lon)
    lon_b = lax.ppermute(cols_b, axes, pairs_b)
    lon_a = lax.ppermute(cols_a, axes, pairs_a)
    strips, inner = call(
        rows_strip_kernel,
        [inner, inner_geo, rims, got_a, got_b, hinge],
        [(4, 2 * HALO) + tile, (4, ROWS + 2) + tile],
        state_scratch(NS_ROWS) + geo_scratch(NS_ROWS),
        smem_last=True,
        flops=10_000_000,
    )
    outs = call(
        columns_strip_kernel,
        [own, lon_b, lon_a, got_a, got_b, inner, strips, hinge],
        [(LEVELS, ROWS, LANES)] * 5,
        state_scratch(WE_ROWS)
        + geo_scratch(WE_ROWS)
        + [pltpu.VMEM((LEVELS, ROWS, LANES), F32)] * 5
        + [pltpu.SemaphoreType.DMA((5, 4))],
        out_far=True,
        smem_last=True,
        flops=10_000_000,
    )
    return tuple(outs)


def solution(mesh):
    field = P(None, "lat", "lon")
    flat = P("lat", "lon")
    return jax.shard_map(
        on_device,
        mesh=mesh,
        in_specs=(field, field, field, field, flat, flat, field, field, P()),
        out_specs=(field,) * 5,
        check_vma=False,
    )
```

```python
import jax
import jax.numpy as jnp
from jax import lax
from jax.experimental import pallas as pl
from jax.experimental.pallas import tpu as pltpu
from jax.sharding import PartitionSpec as P

F32 = jnp.float32
NSTEP = 4
LEVELS = 8
ROWS = 64
LANES = 128
HALO = 4
BLOCK = 9
GROUP = 16

time_step = 0.2
diffusivity = 0.4
eos_alpha = 0.1655
eos_beta = 0.76554
eos_lambda_one = 0.05952
eos_lambda_two = 0.00054914
eos_mu_one = 0.0001497
eos_mu_two = 1.109e-05
eos_cross = 0.0024341

SIGNS = (1.0, 1.0, -1.0, -1.0)


def roll(x, shift):
    shift = shift % LANES
    return pltpu.roll(x, shift, 1) if shift else x


def lanes():
    return lax.broadcasted_iota(jnp.int32, (LEVELS, LANES), 1)


def levels():
    return lax.broadcasted_iota(jnp.int32, (LEVELS, LANES), 0)


def mirrored(x, width):
    return jnp.take_along_axis(x, lanes() ^ (width - 1), axis=1, mode="promise_in_bounds")


def eos_terms():
    depth = 100.0 * (levels().astype(F32) + 0.5)
    return -eos_alpha * (1.0 + eos_mu_one * depth), eos_beta * (1.0 - eos_mu_two * depth)


def density_of(heat, salt, terms):
    heat_term, salt_term = terms
    return heat * (heat_term - (0.5 * eos_alpha * eos_lambda_one) * heat - eos_cross * salt) + salt * (
        salt_term - (0.5 * eos_beta * eos_lambda_two) * salt
    )


def pressure_of(heat, salt, half_depth, terms):
    half = density_of(heat, salt, terms) * half_depth
    level = levels()
    total = half
    for shift in (1, 2, 4):
        total = total + jnp.where(level >= shift, pltpu.roll(total, shift, 0), 0.0)
    return total + total - half


def geometry_row(geo, row, east0, north0, east1, north1):
    half0 = geo["half"][row]
    half1 = geo["half"][row + 1]
    half_e = roll(half0, -1)
    span = 2.0 / (east0 + roll(east0, -1))
    side = 0.5 * (north0 + roll(north0, -1))
    open_e = jnp.minimum(half0, half_e) > 0.0
    area = jnp.where(open_e, side * (half0 + half_e), 0.0)
    geo["area_e"][row] = area
    geo["cond_e"][row] = diffusivity * area * span
    geo["open_e"][row] = jnp.where(open_e, 1.0, 0.0)
    geo["push_e"][row] = time_step * span
    span = 2.0 / (north0 + north1)
    side = 0.5 * (east0 + east1)
    open_n = jnp.minimum(half0, half1) > 0.0
    area = jnp.where(open_n, side * (half0 + half1), 0.0)
    geo["area_n"][row] = area
    geo["cond_n"][row] = diffusivity * area * span
    geo["open_n"][row] = jnp.where(open_n, 1.0, 0.0)
    geo["push_n"][row] = time_step * span
    geo["inv"][row] = (0.5 * time_step) / (east0 * north0 * jnp.where(half0 > 0.0, half0, 1.0))


def march(state, geo, chains, target=None):
    terms = eos_terms()

    def north_face(row, speed):
        flow = geo["area_n"][row] * speed
        ahead = jnp.maximum(flow, 0.0) + geo["cond_n"][row]
        return ahead, flow - ahead

    def begin(row):
        before = tuple(ref[row - 1] for ref in state)
        here = tuple(ref[row] for ref in state)
        return before + here + north_face(row - 1, before[3]) + (pressure_of(here[0], here[1], geo["half"][row], terms),)

    def advance(row, carry):
        before, here = carry[0:4], carry[4:8]
        south_p, south_m, press = carry[8:]
        north = tuple(ref[row + 1] for ref in state)
        press_n = pressure_of(north[0], north[1], geo["half"][row + 1], terms)
        north_p, north_m = north_face(row, here[3])
        flow = geo["area_e"][row] * here[2]
        east_p = jnp.maximum(flow, 0.0) + geo["cond_e"][row]
        east_m = flow - east_p
        west_p, west_m = roll(east_p, 1), roll(east_m, 1)
        inv = geo["inv"][row]
        keep = 1.0 - inv * ((east_p - west_m) + (north_p - south_m))
        c_e, c_w, c_n, c_s = inv * east_m, inv * west_p, inv * north_m, inv * south_p
        new = [
            keep * c + (c_w * roll(c, 1) + c_s * s) - (c_e * roll(c, -1) + c_n * n)
            for c, s, n in zip(here, before, north)
        ]
        new[2] = (new[2] + (press - roll(press, -1)) * geo["push_e"][row]) * geo["open_e"][row]
        new[3] = (new[3] + (press - press_n) * geo["push_n"][row]) * geo["open_n"][row]
        for ref, value in zip(state if target is None else target, new):
            ref[row] = value
        return here + north + (north_p, north_m, press_n)

    carries = [begin(first) for first, _ in chains]
    for u in range(max(count for _, count in chains)):
        for index, (first, count) in enumerate(chains):
            if u < count:
                carries[index] = advance(first + u, carries[index])


GEO = ("half", "area_e", "cond_e", "open_e", "push_e", "area_n", "cond_n", "open_n", "push_n", "inv")


def geo_scratch(rows):
    return [pltpu.VMEM((rows, LEVELS, LANES), F32) for _ in GEO]


def column_of(ref, row):
    return ref[pl.ds(row, LEVELS, stride=ref.shape[0] // LEVELS), :]


def wide(ref, row):
    return jnp.broadcast_to(ref[pl.ds(row, 1), :], (LEVELS, LANES))


def own_row(refs, row):
    heat, salt, east, north, thick, water = [column_of(ref, row) for ref in refs[:6]]
    wet = water.astype(F32)
    return heat * wet, salt * wet, east, north, 0.5 * (thick * wet)


def rows_kernel(*refs):
    ins, (out_a, out_b) = refs[:8], refs[8:10]
    rims, sems = refs[10:18], refs[18]
    copies = []
    for f, (src, dst) in enumerate(zip(ins, rims)):
        for side, row in ((0, 0), (1, ROWS - 8)):
            if f < 6:
                pair = src.at[:, pl.ds(row, 8), :], dst.at[side]
            else:
                pair = src.at[pl.ds(row, 8), :], dst.at[side]
            copies.append(pltpu.make_async_copy(*pair, sems.at[f, side]))
    for copy in copies:
        copy.start()
    for i in range(20, 27):
        out_a[i] = jnp.ones((LEVELS, LANES), F32)
    out_b[25] = jnp.ones((LEVELS, LANES), F32)
    out_b[26] = jnp.ones((LEVELS, LANES), F32)
    for copy in copies:
        copy.wait()
    even = lax.rem(lax.axis_index("lat"), 2) == 0
    side_a = jnp.where(even, 1, 0)
    row_a = jnp.where(even, HALO, 0)
    side_b = jnp.where(even, 0, 1)
    row_b = jnp.where(even, 0, HALO - 1)
    for out, side, row, count, flat in ((out_a, side_a, row_a, HALO, 0), (out_b, side_b, row_b, HALO + 1, 1)):
        cut = [ref.at[side].reshape(LEVELS * 8, LANES) for ref in rims[:6]]
        for i in range(count):
            for f, value in enumerate(own_row(cut, row + i)):
                out[5 * i + f] = value
            for f in range(2):
                place = (20, HALO * f + i) if flat == 0 else (25 + f, i)
                out[place[0], pl.ds(place[1], 1), :] = rims[6 + f][side, pl.ds(row + i, 1), :]


def halo_rows(got_a, got_b):
    even = lax.rem(lax.axis_index("lat"), 2) == 0

    def spread(row):
        return jnp.broadcast_to(row, (LEVELS, LANES))

    def read_a(i, f):
        if f < 5:
            return got_a[5 * i + f]
        return spread(got_a[20, pl.ds(HALO * (f - 5) + i, 1), :])

    def read_b(i, f):
        if f < 5:
            return got_b[5 * i + f]
        return spread(got_b[20 + f, pl.ds(i, 1), :])

    def sane(value, f):
        return value if f < 5 else jnp.where(value > 0.0, value, 1.0)

    def south(i, f):
        return sane(jnp.where(even, read_b(i + 1, f), read_a(i, f)), f)

    def north(i, f):
        return sane(jnp.where(even, read_a(i, f), read_b(i, f)), f)

    def fold(i, f):
        return sane(read_b(i, f), f)

    return south, north, fold


def interior_kernel(*refs):
    ins = refs[:8]
    state_out, own, msgs, rims, geo_out = refs[8:13]
    state = [state_out.at[f] for f in range(4)]
    geo = {name: geo_out.at[index] for index, name in enumerate(GEO)}
    spread = refs[13:15]
    blank = jnp.zeros((LEVELS, LANES), F32)
    for ref in state + [geo["half"]]:
        ref[0] = blank
        ref[ROWS + 1] = blank

    def take(row, carry):
        values = own_row(ins, row)
        for ref, value in zip(state, values):
            ref[row + 1] = value
        geo["half"][row + 1] = values[4]
        spread[0][row + 1] = wide(ins[6], row)
        spread[1][row + 1] = wide(ins[7], row)
        return carry

    lax.fori_loop(0, ROWS, take, 0, unroll=8)
    for i in range(8):
        for place, row in ((i, i), (8 + i, ROWS - 8 + i)):
            for f in range(4):
                rims[f, place] = state[f][row + 1]
            rims[4, place] = geo["half"][row + 1]
            rims[5, place] = spread[0][row + 1]
            rims[6, place] = spread[1][row + 1]

    lane = lanes()
    part = (lane >> 2) & 3

    def pack(g, carry):
        packs = []
        for f in range(7):
            west = east = jnp.zeros((LEVELS, LANES), F32)
            for q in range(8):
                row = jnp.clip(BLOCK * q + g - HALO, 0, ROWS - 1)
                if f < 4:
                    value = state[f][row + 1]
                elif f == 4:
                    value = geo["half"][row + 1]
                else:
                    value = spread[f - 5][row + 1]
                here = (lane >> 4) == q
                west = jnp.where(here, roll(value, GROUP * q + HALO), west)
                east = jnp.where(here, roll(value, GROUP * q + 12), east)
            own[0, f, g] = west
            own[1, f, g] = east
            packs.append((west, east))
        for side in range(2):
            for half, first in ((0, 0), (1, 4)):
                message = jnp.zeros((LEVELS, LANES), F32)
                for f in range(4 if half == 0 else 3):
                    value = packs[first + f][side]
                    shift = HALO * f - (HALO if side == 0 else 2 * HALO)
                    message = jnp.where(part == f, roll(value, shift), message)
                msgs[side, BLOCK * half + g] = message
        return carry

    lax.fori_loop(0, BLOCK, pack, 0, unroll=3)

    def shape(row, carry):
        geometry_row(geo, row + 1, spread[0][row + 1], spread[1][row + 1], spread[0][row + 2], spread[1][row + 2])
        return carry

    lax.fori_loop(0, ROWS - 1, shape, 0, unroll=7)

    def step(s, carry):
        march(state, geo, ((2, ROWS - 2),))
        return carry

    lax.fori_loop(1, NSTEP - 1, step, 0)


def columns_kernel(msgs, got_a, got_b, out_a, out_b):
    even = lax.rem(lax.axis_index("lon"), 2) == 0
    top = lax.axis_index("lat") == lax.axis_size("lat") - 1
    south, north, fold = halo_rows(got_a, got_b)
    lane = lanes()
    part = (lane >> 2) & 3
    for half, first in ((0, 0), (1, 4)):
        for g in range(BLOCK):
            slot = BLOCK * half + g
            west, east = msgs[0, slot], msgs[1, slot]
            if g != HALO:
                add_w = add_e = jnp.zeros((LEVELS, LANES), F32)
                base = 0 if g < HALO else 7 * GROUP
                for f in range(4 if half == 0 else 3):
                    if g < HALO:
                        value = south(g, first + f)
                    else:
                        value = jnp.where(top, fold(g - 4, first + f), north(g - 5, first + f))
                    add_w = jnp.where(part == f, roll(value, base + HALO * f), add_w)
                    add_e = jnp.where(part == f, roll(value, base + HALO * f + HALO), add_e)
                if g < HALO:
                    here = lane < GROUP
                else:
                    here = lane >= 7 * GROUP
                    add_w, add_e = jnp.where(top, add_e, add_w), jnp.where(top, add_w, add_e)
                west = jnp.where(here, add_w, west)
                east = jnp.where(here, add_e, east)
            out_a[slot] = jnp.where(even, east, west)
            out_b[slot] = jnp.where(even, west, east)


SOUTH, NORTH, FOLD, NS_ROWS = 0, 12, 24, 30


def rows_strip_kernel(*refs):
    inner, inner_geo, rims, got_a, got_b, hinge, out = refs[:7]
    state = refs[7:11]
    east_w, north_w = refs[11:13]
    geo = dict(zip(GEO, refs[13:]))
    top = lax.axis_index("lat") == lax.axis_size("lat") - 1
    pivot = hinge[0]
    south, north, fold = halo_rows(got_a, got_b)
    fields = list(state) + [geo["half"], east_w, north_w]
    for f, ref in enumerate(fields):
        for i in range(HALO):
            ref[SOUTH + i] = south(i, f)
            ref[NORTH + 8 + i] = north(i, f)
            ref[FOLD + i] = fold(i, f)
        ref[FOLD + HALO] = fold(HALO, f)
        for i in range(8):
            ref[SOUTH + HALO + i] = rims[f, i]
            ref[NORTH + i] = rims[f, 8 + i]

    def refold(ref, sign):
        ghost = sign * mirrored(ref[FOLD + 4 - pivot], LANES)
        ref[FOLD + 5] = sign * mirrored(ref[NORTH + 7 - pivot], LANES)
        ref[NORTH + 8] = jnp.where(top, ghost, ref[NORTH + 8])

    for ref in fields[4:]:
        refold(ref, 1.0)
    for row in (*range(SOUTH, SOUTH + 11), *range(NORTH, NORTH + 11), *range(FOLD, FOLD + 5)):
        geometry_row(geo, row, east_w[row], north_w[row], east_w[row + 1], north_w[row + 1])

    for s in range(1, NSTEP + 1):
        for ref, sign in zip(state, SIGNS):
            refold(ref, sign)
        chains = [(SOUTH + s, 12 - 2 * s), (NORTH + s, 12 - 2 * s)]
        if s < NSTEP:
            chains.append((FOLD + s, 5 - s))
        march(state, geo, chains)

    held = [out.at[f] for f in range(4)]
    held_geo = {name: inner_geo.at[index] for index, name in enumerate(GEO)}
    for f, ref in enumerate(held):
        for row in range(HALO - 1, ROWS - HALO + 3):
            ref[row] = inner[f, row]

    def last(s, carry):
        march(held, held_geo, ((HALO, ROWS - 2 * HALO + 2),))
        return carry

    lax.fori_loop(NSTEP - 1, NSTEP + 1, last, 0)

    for f, ref in enumerate(state):
        for i in range(HALO):
            out[f, 1 + i] = ref[SOUTH + HALO + i]
            out[f, 1 + ROWS - HALO + i] = ref[NORTH + HALO + i]


WEST, EAST, FOLDS, WE_ROWS = 0, 11, 22, 28


def columns_strip_kernel(*refs):
    own, lon_b, lon_a, got_a, got_b, inner, hinge = refs[:7]
    outs = refs[7:12]
    state = refs[12:16]
    east_w, north_w = refs[16:18]
    geo = dict(zip(GEO, refs[18:28]))
    stage, sems = refs[28:33], refs[33]
    even = lax.rem(lax.axis_index("lon"), 2) == 0
    top = lax.axis_index("lat") == lax.axis_size("lat") - 1
    below = hinge[0] == 1
    south, north, fold = halo_rows(got_a, got_b)
    fields = list(state) + [geo["half"], east_w, north_w]
    lane = lanes()
    inside = lane & (GROUP - 1)

    def message(side, f, g):
        slot = g if f < 4 else BLOCK + g
        a, b = lon_a[slot], lon_b[slot]
        return jnp.where(even, b, a) if side == 0 else jnp.where(even, a, b)

    for g in range(BLOCK):
        for f, ref in enumerate(fields):
            west, east = own[0, f, g], own[1, f, g]
            if g < HALO:
                value = south(g, f)
                west = jnp.where(lane < GROUP, roll(value, HALO), west)
                east = jnp.where(lane < GROUP, roll(value, 12), east)
            elif g > HALO:
                value = north(g - 5, f)
                west = jnp.where(lane >= 7 * GROUP, roll(value, 7 * GROUP + HALO), west)
                east = jnp.where(lane >= 7 * GROUP, roll(value, 7 * GROUP + 12), east)
            shift = -HALO * (f % 4)
            west = jnp.where(inside < HALO, roll(message(0, f, g), shift), west)
            east = jnp.where(inside >= 12, roll(message(1, f, g), shift + 12), east)
            if f > 4:
                west = jnp.where(west > 0.0, west, 1.0)
                east = jnp.where(east > 0.0, east, 1.0)
            ref[WEST + 1 + g] = west
            ref[EAST + 1 + g] = east

    def rewrap(ref):
        for base in (WEST, EAST):
            ref[base] = roll(ref[base + 9], GROUP)
            ref[base + 10] = roll(ref[base + 1], -GROUP)

    def refold(ref, sign):
        ghost = sign * mirrored(jnp.where(below, ref[FOLDS + 3], ref[FOLDS + 4]), GROUP)
        from_e = jnp.where(below, ref[EAST + 4], ref[EAST + 5])
        from_w = jnp.where(below, ref[WEST + 4], ref[WEST + 5])
        back = jnp.where(lane < GROUP, roll(from_e, GROUP), roll(from_w, 2 * GROUP))
        ref[FOLDS + 5] = sign * mirrored(back, GROUP)
        here = (lane >= 7 * GROUP) & top
        ref[WEST + 6] = jnp.where(here, roll(ghost, 6 * GROUP), ref[WEST + 6])
        ref[EAST + 6] = jnp.where(here, roll(ghost, 7 * GROUP), ref[EAST + 6])

    for i in range(HALO + 1):
        for f, ref in enumerate(fields):
            value = fold(i, f)
            value = jnp.where(lane < GROUP, roll(value, HALO), roll(value, 28))
            if i > 0:
                slot = HALO + i
                corner = 7 * GROUP + HALO * (f % 4)
                value = jnp.where(lane < HALO, roll(message(1, f, slot), -corner), value)
                other = roll(message(0, f, slot), 28 - corner)
                value = jnp.where((lane >= 28) & (lane < 32), other, value)
            if f > 4:
                value = jnp.where(value > 0.0, value, 1.0)
            ref[FOLDS + i] = value
    for ref in fields[4:]:
        refold(ref, 1.0)
        rewrap(ref)
    for row in (*range(WEST, WEST + 10), *range(EAST, EAST + 10), *range(FOLDS, FOLDS + 5)):
        geometry_row(geo, row, east_w[row], north_w[row], east_w[row + 1], north_w[row + 1])

    def step(s, carry):
        for ref, sign in zip(state, SIGNS):
            refold(ref, sign)
            rewrap(ref)
        march(state, geo, ((WEST + 1, BLOCK), (EAST + 1, BLOCK), (FOLDS + 1, 4)))
        return carry

    lax.fori_loop(1, NSTEP + 1, step, 0)

    for ref in state:
        for g in range(BLOCK):
            ref[WEST + 1 + g] = jnp.where(inside < HALO, roll(ref[EAST + 1 + g], -8), ref[WEST + 1 + g])
    rim = (lane < HALO) | (lane >= LANES - HALO)
    terms = eos_terms()

    copies = []
    for row in range(ROWS):
        q, g = divmod(row + HALO, BLOCK)
        bases = [inner[f, row + 1] for f in range(4)]
        new = [
            jnp.where(rim, roll(ref[WEST + 1 + g], -(GROUP * q + HALO)), base) for ref, base in zip(state, bases)
        ]
        new.append(density_of(new[0], new[1], terms))
        for ref, value in zip(stage, new):
            ref.reshape(LEVELS * ROWS, LANES)[pl.ds(row, LEVELS, stride=ROWS), :] = value
        if row % 16 == 15:
            rows = pl.ds(row - 15, 16)
            for f in range(5):
                copy = pltpu.make_async_copy(stage[f].at[:, rows, :], outs[f].at[:, rows, :], sems.at[f, row // 16])
                copy.start()
                copies.append(copy)
    for copy in copies:
        copy.wait()


def call(kernel, ins, outs, scratch=(), smem_last=False, far=False, out_far=False, flops=0):
    place = pltpu.HBM if far else pltpu.VMEM
    specs = [pl.BlockSpec(memory_space=place) for _ in ins]
    ins = [pltpu.with_memory_space_constraint(x, place) for x in ins[:-1]] + [ins[-1]]
    if smem_last:
        specs[-1] = pl.BlockSpec(memory_space=pltpu.SMEM)
    else:
        ins[-1] = pltpu.with_memory_space_constraint(ins[-1], place)
    if out_far:
        out_shape = [jax.ShapeDtypeStruct(shape, F32) for shape in outs]
    else:
        out_shape = [pltpu.VMEM(shape, F32) for shape in outs]
    return pl.pallas_call(
        kernel,
        out_shape=out_shape,
        in_specs=specs,
        out_specs=[pl.BlockSpec(memory_space=pltpu.HBM if out_far else pltpu.VMEM) for _ in outs],
        scratch_shapes=list(scratch),
        compiler_params=pltpu.CompilerParams(vmem_limit_bytes=40 * 1024 * 1024),
        cost_estimate=pl.CostEstimate(flops=flops, bytes_accessed=2_000_000, transcendentals=0),
    )(*ins)


def lat_pairs(lat, lon):
    first = [(a * lon + o, (a ^ 1) * lon + o) for a in range(lat) for o in range(lon)]
    second = [
        (a * lon + o, (a + 1 if a % 2 else a - 1) * lon + o) for a in range(1, lat - 1) for o in range(lon)
    ]
    second += [((lat - 1) * lon + o, (lat - 1) * lon + lon - 1 - o) for o in range(lon)]
    return first, second


def lon_pairs(lat, lon):
    first = [(a * lon + o, a * lon + (o ^ 1)) for a in range(lat) for o in range(lon)]
    second = [
        (a * lon + o, a * lon + ((o + 1) if o % 2 else (o - 1)) % lon) for a in range(lat) for o in range(lon)
    ]
    return first, second


def on_device(*args):
    lat, lon = lax.axis_size("lat"), lax.axis_size("lon")
    axes = ("lat", "lon")
    hinge = args[8]
    tile = (LEVELS, LANES)
    fields = [*args[:4], args[6], args[7], args[4], args[5]]
    flat = [x.reshape(LEVELS * ROWS, LANES) for x in fields[:6]] + fields[6:]
    kinds = [F32] * 5 + [jnp.int32] + [F32] * 2
    state_scratch = lambda rows: [pltpu.VMEM((rows,) + tile, F32) for _ in range(6)]

    rows_a, rows_b = call(
        rows_kernel,
        fields,
        [(27,) + tile, (27,) + tile],
        [pltpu.VMEM((2, LEVELS) + tile, kind) for kind in kinds[:6]]
        + [pltpu.VMEM((2,) + tile, F32)] * 2
        + [pltpu.SemaphoreType.DMA((8, 2))],
        far=True,
    )
    pairs_a, pairs_b = lat_pairs(lat, lon)
    got_b = lax.ppermute(rows_b, axes, pairs_b)
    got_a = lax.ppermute(rows_a, axes, pairs_a)
    inner, own, msgs, rims, inner_geo = call(
        interior_kernel,
        flat,
        [(4, ROWS + 2) + tile, (2, 7, BLOCK) + tile, (2, 2 * BLOCK) + tile, (7, 16) + tile, (len(GEO), ROWS + 2) + tile],
        [pltpu.VMEM((ROWS + 2,) + tile, F32)] * 2,
        flops=40_000_000,
    )
    cols_a, cols_b = call(columns_kernel, [msgs, got_a, got_b], [(2 * BLOCK,) + tile] * 2)
    pairs_a, pairs_b = lon_pairs(lat, lon)
    lon_b = lax.ppermute(cols_b, axes, pairs_b)
    lon_a = lax.ppermute(cols_a, axes, pairs_a)
    (inner,) = call(
        rows_strip_kernel,
        [inner, inner_geo, rims, got_a, got_b, hinge],
        [(4, ROWS + 2) + tile],
        state_scratch(NS_ROWS) + geo_scratch(NS_ROWS),
        smem_last=True,
        flops=10_000_000,
    )
    outs = call(
        columns_strip_kernel,
        [own, lon_b, lon_a, got_a, got_b, inner, hinge],
        [(LEVELS, ROWS, LANES)] * 5,
        state_scratch(WE_ROWS)
        + geo_scratch(WE_ROWS)
        + [pltpu.VMEM((LEVELS, ROWS, LANES), F32)] * 5
        + [pltpu.SemaphoreType.DMA((5, 4))],
        out_far=True,
        smem_last=True,
        flops=10_000_000,
    )
    return tuple(outs)


def solution(mesh):
    field = P(None, "lat", "lon")
    flat = P("lat", "lon")
    return jax.shard_map(
        on_device,
        mesh=mesh,
        in_specs=(field, field, field, field, flat, flat, field, field, P()),
        out_specs=(field,) * 5,
        check_vma=False,
    )
```
